128 devices in a mesh: ctx: 64 (over z, x_hi, y, core), fsdp: 2 (over x_lo).
Axes of the slice: x: 4 (x_hi: 2, x_lo: 2; x = x_hi * 2 + x_lo), y: 4, z: 4, core: 2. Of those that a mesh axis runs over, the one named last changes fastest.
Arguments:
- tokens: bfloat16 [16384, 768], P(('ctx', 'fsdp')), may hold values from -100 to 100
- block_order: int32 [128], replicated, may hold values from 0 to 127, each once
- cotangent: bfloat16 [16384, 768], P(('ctx', 'fsdp')), may hold values from -6 to 6
- ln_gain_attn: bfloat16 [768], P('fsdp'), may hold values from 0.099609375 to 1.8984375
- ln_bias_attn: bfloat16 [768], P('fsdp'), may hold values from -1.5 to 1.5
- ln_gain_mlp: bfloat16 [768], P('fsdp'), may hold values from 0.099609375 to 1.8984375
- ln_bias_mlp: bfloat16 [768], P('fsdp'), may hold values from -1.5 to 1.5
- w_qkv: bfloat16 [768, 2304], P('fsdp'), may hold values from -0.21875 to 0.21875
- b_qkv: bfloat16 [2304], P('fsdp'), may hold values from -1.5 to 1.5
- w_out: bfloat16 [768, 768], P('fsdp'), may hold values from -2.5 to 2.5
- b_out: bfloat16 [768], P('fsdp'), may hold values from -1.5 to 1.5
- w_fc1: bfloat16 [768, 3072], P('fsdp'), may hold values from -0.21875 to 0.21875
- b_fc1: bfloat16 [3072], P('fsdp'), may hold values from -1.5 to 1.5
- w_fc2: bfloat16 [3072, 768], P('fsdp'), may hold values from -0.109375 to 0.109375
- b_fc2: bfloat16 [768], P('fsdp'), may hold values from -1.5 to 1.5
Outputs:
- layer_out: bfloat16 [16384, 768], P(('ctx', 'fsdp'))
- grad_tokens: float32 [16384, 768], P(('ctx', 'fsdp'))
- grad_ln_gain_attn: float32 [768], P('fsdp')
- grad_ln_bias_attn: float32 [768], P('fsdp')
- grad_ln_gain_mlp: float32 [768], P('fsdp')
- grad_ln_bias_mlp: float32 [768], P('fsdp')
- grad_w_qkv: float32 [768, 2304], P('fsdp')
- grad_b_qkv: float32 [2304], P('fsdp')
- grad_w_out: float32 [768, 768], P('fsdp')
- grad_b_out: float32 [768], P('fsdp')
- grad_w_fc1: float32 [768, 3072], P('fsdp')
- grad_b_fc1: float32 [3072], P('fsdp')
- grad_w_fc2: float32 [3072, 768], P('fsdp')
- grad_b_fc2: float32 [768], P('fsdp')
The draws below stay inside these ranges and needn't reach their ends.
All inputs are finite; a program needn't handle non-finite values.
Results may differ from the reference program's by a relative error of at most 0.0095.
Values may be sent and summed in bfloat16 or wider, within the bound.
No kernel may reach another device: no remote copies, remote signals or barrier semaphores. Data moves between devices by JAX's collectives and lax.ppermute only.
A program may use at most 512 MiB of HBM per device.

```python
import math
import jax
import jax.numpy as jnp
from jax import lax

D = 768
HEADS = 12
HEAD = 64
ROT = 16
FF = 3072
TOK_DEV = 128
NBLK = 128
SEQ = 16384


def draw_tokens(key, part):
    key = jax.random.fold_in(key, 11)
    key_rows, key_cols, key_vals = jax.random.split(key, 3)
    row_scale = jnp.exp(jax.random.uniform(key_rows, (SEQ, 1), jnp.float32, 0.0, math.log(10.0)))
    col_scale = jnp.exp(jax.random.uniform(key_cols, (1, D), jnp.float32, math.log(0.5), math.log(2.0)))
    values = jnp.clip(jax.random.normal(key_vals, (SEQ, D), jnp.float32), -5.0, 5.0)
    return (values * row_scale * col_scale).astype(jnp.bfloat16)


def levels(rng, dims, pieces, low, top_value):
    level = 1.0
    for axis_at, blocks in pieces:
        heights = jax.random.uniform(jax.random.fold_in(jax.random.fold_in(rng, 6), axis_at), (blocks,), jnp.float32, low / len(pieces), top_value / len(pieces))
        level = level * jnp.repeat(jnp.exp(heights), dims[axis_at] // blocks).reshape((-1,) + (1,) * (len(dims) - 1 - axis_at))
    return level


def noise(own_key, dims, spread, limit, pieces=(), held_as=jnp.bfloat16):
    array = jax.random.normal(own_key, dims, jnp.float32) * spread
    if len(pieces) > 0:
        array = levels(own_key, dims, pieces, -0.22, 0.18) * array
    return jnp.clip(array, min=-limit, max=limit).astype(held_as)


def setup_inputs(seed: int = 0) -> dict:
    seeds = jax.random.split(jax.random.key(seed), 16)
    return {
        "tokens": draw_tokens(jax.random.fold_in(seeds[15], 71), 0),
        "block_order": jax.random.permutation(seeds[1], NBLK).astype(jnp.int32),
        "cotangent": noise(seeds[2], (SEQ, D), 1.0, 6.0, ((0, 128),)),
        "ln_gain_attn": jnp.clip(1.0 + 0.18 * jax.random.normal(seeds[3], (D,), jnp.float32), 0.099609375, 1.8984375).astype(jnp.bfloat16),
        "ln_bias_attn": noise(seeds[4], (D,), 0.3, 1.5, ((0, 2),)),
        "ln_gain_mlp": jnp.clip(1.0 + 0.18 * jax.random.normal(seeds[5], (D,), jnp.float32), 0.099609375, 1.8984375).astype(jnp.bfloat16),
        "ln_bias_mlp": noise(seeds[6], (D,), 0.3, 1.5, ((0, 2),)),
        "w_qkv": noise(seeds[7], (D, 3 * D), D ** -0.5, 0.21875, ((0, 2),)),
        "b_qkv": noise(seeds[8], (3 * D,), 0.3, 1.5, ((0, 2),)),
        "w_out": noise(seeds[9], (D, D), (max(1, D * 128 // SEQ)) ** -0.5, 2.5, ((0, 2),)),
        "b_out": noise(seeds[10], (D,), 0.3, 1.5, ((0, 2),)),
        "w_fc1": noise(seeds[11], (D, FF), D ** -0.5, 0.21875, ((0, 2),)),
        "b_fc1": noise(seeds[12], (FF,), 0.3, 1.5, ((0, 2),)),
        "w_fc2": noise(seeds[13], (FF, D), FF ** -0.5, 0.109375, ((0, 2),)),
        "b_fc2": noise(seeds[14], (D,), 0.3, 1.5, ((0, 2),)),
    }


EPS = 1e-05
MASKED = -1e+30

@jax.custom_vjp
def low(v):
    return lax.optimization_barrier(v.astype(jnp.bfloat16)).astype(jnp.float32)

@jax.custom_vjp
def low_back(v):
    return v

def low_keep(v):
    return (low(v), None)

def low_pass(kept, grad):
    return (grad,)

def back_keep(v):
    return (v, None)

def back_low(kept, grad):
    return (low(grad),)
low.defvjp(low_keep, low_pass)
low_back.defvjp(back_keep, back_low)

def rotate(vectors, places, direction):
    half_dims = ROT // 2
    frequency = jnp.exp(jnp.arange(half_dims, dtype=jnp.float32) * (-2.0 * math.log(10000.0) / ROT))
    angles = places.astype(jnp.float32)[:, None] * frequency[None, :]
    cosine = jnp.cos(angles)[:, None, :]
    sines = direction * jnp.sin(angles)[:, None, :]
    first_half = vectors[..., :half_dims]
    second_half = vectors[..., half_dims:ROT]
    return jnp.concatenate([first_half * cosine - second_half * sines, second_half * cosine + first_half * sines, vectors[..., ROT:]], axis=-1)

def norms(inputs, gain_attn, bias_attn, gain_mlp, bias_mlp):
    row_mean = lax.optimization_barrier(jnp.mean(inputs, axis=1, keepdims=True))
    centred = inputs - row_mean
    row_var = lax.optimization_barrier(jnp.mean(centred * centred, axis=1, keepdims=True))
    normed = centred * lax.rsqrt(row_var + EPS)
    return (normed * gain_attn + bias_attn, normed * gain_mlp + bias_mlp)

def reference(tokens, block_order, cotangent, ln_gain_attn, ln_bias_attn, ln_gain_mlp, ln_bias_mlp, w_qkv, b_qkv, w_out, b_out, w_fc1, b_fc1, w_fc2, b_fc2):
    row_index = jnp.arange(SEQ, dtype=jnp.int32)
    places = block_order[row_index // TOK_DEV] * TOK_DEV + row_index % TOK_DEV
    span = min(512, SEQ)
    score_scale = 1.0 / math.sqrt(HEAD)

    def matmul(left, right):
        return jnp.dot(left, right, precision=lax.Precision.HIGHEST)

    def forward(inputs, gain_attn, bias_attn, gain_mlp, bias_mlp, weight_qkv, bias_qkv, weight_out, bias_out, weight_one, bias_one, weight_two, bias_two):
        h_attn, h_mlp = norms(inputs, gain_attn, bias_attn, gain_mlp, bias_mlp)
        a_attn = low(h_attn)
        a_mlp = low(h_mlp)
        qkv_all = low_back(matmul(a_attn, weight_qkv) + bias_qkv)
        queries = low(rotate(qkv_all[:, :D].reshape(SEQ, HEADS, HEAD), places, 1.0))
        keys_all = low(rotate(qkv_all[:, D:2 * D].reshape(SEQ, HEADS, HEAD), places, 1.0))
        values_all = low(qkv_all[:, 2 * D:].reshape(SEQ, HEADS, HEAD))

        def attend(blocks):
            query_block, block_places = blocks
            scores = low_back(jnp.einsum('qhd,khd->qhk', query_block, keys_all, precision=lax.Precision.HIGHEST) * score_scale)
            allowed = places[None, None, :] <= block_places[:, None, None]
            scores = jnp.where(allowed, scores, MASKED)
            peak = lax.optimization_barrier(jnp.max(scores, axis=2, keepdims=True))
            exps = jnp.exp(scores - peak)
            probs = low(exps / lax.optimization_barrier(jnp.sum(exps, axis=2, keepdims=True)))
            return jnp.einsum('qhk,khd->qhd', probs, values_all, precision=lax.Precision.HIGHEST)
        attended = lax.map(jax.checkpoint(attend), (queries.reshape(SEQ // span, span, HEADS, HEAD), places.reshape(SEQ // span, span)))
        mixed_heads = low_back(low(attended.reshape(SEQ, D)))
        attn_out = matmul(mixed_heads, weight_out) + bias_out
        hidden_pre = low_back(matmul(a_mlp, weight_one) + bias_one)
        hidden_act = low(jax.nn.gelu(hidden_pre, approximate=False))
        return inputs + attn_out + matmul(hidden_act, weight_two) + bias_two
    floats = tuple((member.astype(jnp.float32) for member in (tokens, ln_gain_attn, ln_bias_attn, ln_gain_mlp, ln_bias_mlp, w_qkv, b_qkv, w_out, b_out, w_fc1, b_fc1, w_fc2, b_fc2)))
    result, pullback = jax.vjp(forward, *floats)
    gradients = pullback(cotangent.astype(jnp.float32))
    return (result.astype(jnp.bfloat16), gradients[0], gradients[1], gradients[2], gradients[3], gradients[4], gradients[5], gradients[6], gradients[7], gradients[8], gradients[9], gradients[10], gradients[11], gradients[12])
```

```python
from functools import partial
import math

import jax
import jax.numpy as jnp
from jax import lax
from jax.experimental import pallas as pl
from jax.experimental.pallas import tpu as pltpu
from jax.sharding import Mesh, PartitionSpec as P

HEADS = 12
HEAD = 64
ROT = 16
D = 768
FF = 3072
BLK = 128
EPS = 1e-05
MASKED = -1e30
FLOOR = -1e20

AXES = ("z", "xh", "y", "core", "fsdp")
SIZES = (4, 2, 4, 2, 2)
CTX = ("z", "xh", "y", "core")
TEAM = ("core", "fsdp")
KEYS = ("z", "xh")
GROUPS = ("z", "xh", "y")

NH = 3
HW = NH * HEAD
TEAM_ROWS = 512
NQ = 16
NK = 32
QT = 2
CH = 4
NT = NQ // QT
BF = jnp.bfloat16
F32 = jnp.float32
VMEM_LIMIT = 56 * 1024 * 1024


def _sort_keys(kv_ref, ksrc, kvt, kn):
    def step(r, _):
        src = ksrc[r]
        at = pl.multiple_of((src % 4) * BLK, BLK)
        to = pl.multiple_of(r * BLK, BLK)
        blk = kv_ref[src // 4, :, pl.ds(at, BLK)]
        kvt[:, pl.ds(to, BLK)] = blk
        for h in range(NH):
            kn[h, pl.ds(to, BLK), :] = blk[2 * HEAD * h : 2 * HEAD * (h + 1)].T
        return 0

    lax.fori_loop(0, NK, step, 0)


def _tile_columns(ref, qsrc, t, rows):
    parts = []
    for i in range(QT):
        src = qsrc[t * QT + i]
        at = pl.multiple_of((src % 4) * BLK, BLK)
        parts.append(ref[src // 4, rows, pl.ds(at, BLK)])
    return jnp.concatenate(parts, axis=1)


def _allowed(kpos, qpos, t, c):
    row = lax.broadcasted_iota(jnp.int32, (BLK, QT * BLK), 0)
    col = lax.broadcasted_iota(jnp.int32, (BLK, BLK), 1)
    query = jnp.concatenate([qpos[t * QT + i] * BLK + col for i in range(QT)], axis=1)
    return jnp.concatenate([kpos[c * CH + i] * BLK + row <= query for i in range(CH)], axis=0)


def _forward(qsrc, qpos, ksrc, kpos, nfull, nall, qd_ref, kv_ref, o_ref, kvt, kn):
    _sort_keys(kv_ref, ksrc, kvt, kn)
    width = QT * BLK
    rows = CH * BLK

    def tile(t, _):
        blk = _tile_columns(qd_ref, qsrc, t, slice(None))
        half = lax.broadcasted_iota(jnp.int32, (2 * HEAD, width), 0) < HEAD
        zero = jnp.zeros((2 * HEAD, width), BF)
        queries = [
            jnp.where(half, blk[2 * HEAD * h : 2 * HEAD * (h + 1)], zero) for h in range(NH)
        ]

        def chunk(masked, c, carry):
            at = pl.multiple_of(c * rows, rows)
            out = []
            if masked:
                ok = _allowed(kpos, qpos, t, c)
            for h in range(NH):
                m, l, acc = carry[h]
                s = jnp.dot(kn[h, pl.ds(at, rows), :], queries[h], preferred_element_type=F32)
                if masked:
                    s = jnp.where(ok, s, MASKED)
                new = jnp.maximum(m, jnp.max(s, axis=0, keepdims=True))
                p = jnp.exp(s - new)
                fade = jnp.exp(m - new)
                l = l * fade + jnp.sum(p, axis=0, keepdims=True)
                v = kvt[2 * HEAD * h + HEAD : 2 * HEAD * (h + 1), pl.ds(at, rows)]
                acc = acc * fade + jnp.dot(v, p.astype(BF), preferred_element_type=F32)
                out.append((new, l, acc))
            return tuple(out)

        start = tuple(
            (
                jnp.full((1, width), FLOOR, F32),
                jnp.zeros((1, width), F32),
                jnp.zeros((HEAD, width), F32),
            )
            for _ in range(NH)
        )
        state = lax.fori_loop(0, nfull[t], partial(chunk, False), start)
        state = lax.fori_loop(nfull[t], nall[t], partial(chunk, True), state)
        stats = []
        for h in range(NH):
            m, l, acc = state[h]
            some = l > 0.0
            safe = jnp.where(some, l, 1.0)
            o = (acc / safe).astype(BF)
            lse = jnp.where(some, m + jnp.log(safe), FLOOR)
            hi = lse.astype(BF)
            rest = lse - hi.astype(F32)
            mid = rest.astype(BF)
            low = (rest - mid.astype(F32)).astype(BF)
            stats += [hi.astype(F32), mid.astype(F32), low.astype(F32)]
            for i in range(QT):
                src = qsrc[t * QT + i]
                at = pl.multiple_of((src % 4) * BLK, BLK)
                o_ref[src // 4, HEAD * h : HEAD * (h + 1), pl.ds(at, BLK)] = o[:, i * BLK : (i + 1) * BLK]
        stats = jnp.concatenate(stats + [jnp.zeros((16 - 3 * NH, width), F32)], axis=0).astype(BF)
        for i in range(QT):
            src = qsrc[t * QT + i]
            at = pl.multiple_of((src % 4) * BLK, BLK)
            o_ref[src // 4, HW : HW + 16, pl.ds(at, BLK)] = stats[:, i * BLK : (i + 1) * BLK]
        return 0

    lax.fori_loop(0, NT, tile, 0)


def _backward(
    qsrc, qpos, ksrc, kpos, nfull, nall, qd_ref, kv_ref, ld_ref, dq_ref, dkv_ref, kvt, kn, acc, w1, w2, dq
):
    _sort_keys(kv_ref, ksrc, kvt, kn)
    width = QT * BLK
    rows = CH * BLK
    acc[...] = jnp.zeros_like(acc)

    def tile(t, _):
        blk = _tile_columns(qd_ref, qsrc, t, slice(None))
        stats = _tile_columns(ld_ref, qsrc, t, slice(None))
        top = lax.broadcasted_iota(jnp.int32, (2 * HEAD, width), 0) < HEAD
        left = lax.broadcasted_iota(jnp.int32, (width, 2 * HEAD), 1) < HEAD
        zero = jnp.zeros((2 * HEAD, width), BF)
        zero_t = jnp.zeros((width, 2 * HEAD), BF)
        for h in range(NH):
            both = blk[2 * HEAD * h : 2 * HEAD * (h + 1)]
            w1[h, :, :width] = jnp.where(top, both, zero)
            w1[h, :, width:] = jnp.where(top, zero, both)
            turned = both.T
            w2[h, :width, :] = jnp.where(left, turned, zero_t)
            w2[h, width:, :] = jnp.where(left, zero_t, turned)
        dq[...] = jnp.zeros_like(dq)

        def chunk(masked, c, _):
            at = pl.multiple_of(c * rows, rows)
            if masked:
                ok = _allowed(kpos, qpos, t, c)
            for h in range(NH):
                sd = jnp.dot(kn[h, pl.ds(at, rows), :], w1[h], preferred_element_type=F32)
                s = sd[:, :width]
                if masked:
                    s = jnp.where(ok, s, MASKED)
                p = jnp.exp(s - stats[h : h + 1])
                ds = (p * (sd[:, width:] - stats[NH + h : NH + h + 1])).astype(BF)
                pd = jnp.concatenate([ds, p.astype(BF)], axis=1)
                acc[h, pl.ds(at, rows), :] += jnp.dot(pd, w2[h], preferred_element_type=F32)
                k = kvt[2 * HEAD * h : 2 * HEAD * h + HEAD, pl.ds(at, rows)]
                dq[h] += jnp.dot(k, ds, preferred_element_type=F32)
            return 0

        lax.fori_loop(0, nfull[t], partial(chunk, False), 0)
        lax.fori_loop(nfull[t], nall[t], partial(chunk, True), 0)
        for h in range(NH):
            out = (dq[h] * 0.125).astype(BF)
            for i in range(QT):
                src = qsrc[t * QT + i]
                at = pl.multiple_of((src % 4) * BLK, BLK)
                dq_ref[src // 4, HEAD * h : HEAD * (h + 1), pl.ds(at, BLK)] = out[:, i * BLK : (i + 1) * BLK]
        return 0

    lax.fori_loop(0, NT, tile, 0)

    def back(r, _):
        src = ksrc[r]
        at = pl.multiple_of((src % 4) * BLK, BLK)
        for h in range(NH):
            part = acc[h, pl.ds(pl.multiple_of(r * BLK, BLK), BLK), :].T.astype(BF)
            dkv_ref[src // 4, 2 * HEAD * h : 2 * HEAD * (h + 1), pl.ds(at, BLK)] = part
        return 0

    lax.fori_loop(0, NK, back, 0)


def _specs(n):
    return [pl.BlockSpec(memory_space=pltpu.VMEM)] * n


def attend_forward(plan, qd, kv):
    return pl.pallas_call(
        _forward,
        out_shape=jax.ShapeDtypeStruct((4, HW + 16, TEAM_ROWS), BF),
        in_specs=[pl.BlockSpec(memory_space=pltpu.SMEM)] * 6 + _specs(2),
        out_specs=pl.BlockSpec(memory_space=pltpu.VMEM),
        scratch_shapes=[
            pltpu.VMEM((2 * HW, NK * BLK), BF),
            pltpu.VMEM((NH, NK * BLK, 2 * HEAD), BF),
        ],
        compiler_params=pltpu.CompilerParams(vmem_limit_bytes=VMEM_LIMIT),
        name="attend_forward",
    )(*plan, qd, kv)


def attend_backward(plan, qd, kv, ld):
    width = QT * BLK
    return pl.pallas_call(
        _backward,
        out_shape=(
            jax.ShapeDtypeStruct((4, HW, TEAM_ROWS), BF),
            jax.ShapeDtypeStruct((8, 2 * HW, TEAM_ROWS), BF),
        ),
        in_specs=[pl.BlockSpec(memory_space=pltpu.SMEM)] * 6 + _specs(3),
        out_specs=tuple(_specs(2)),
        scratch_shapes=[
            pltpu.VMEM((2 * HW, NK * BLK), BF),
            pltpu.VMEM((NH, NK * BLK, 2 * HEAD), BF),
            pltpu.VMEM((NH, NK * BLK, 2 * HEAD), F32),
            pltpu.VMEM((NH, 2 * HEAD, 2 * width), BF),
            pltpu.VMEM((NH, 2 * width, 2 * HEAD), BF),
            pltpu.VMEM((NH, HEAD, width), F32),
        ],
        compiler_params=pltpu.CompilerParams(vmem_limit_bytes=VMEM_LIMIT),
        name="attend_backward",
    )(*plan, qd, kv, ld)


def pick(table, index):
    ids = jnp.arange(table.shape[0], dtype=jnp.int32)
    return jnp.sum(jnp.where(index[:, None] == ids[None, :], table[None, :], 0), axis=1)


def in_order(pos):
    ids = jnp.arange(pos.shape[0], dtype=jnp.int32)
    rank = jnp.sum((pos[None, :] < pos[:, None]).astype(jnp.int32), axis=1)
    hit = rank[None, :] == ids[:, None]
    return (
        jnp.sum(jnp.where(hit, ids[None, :], 0), axis=1),
        jnp.sum(jnp.where(hit, pos[None, :], 0), axis=1),
    )


def make_plan(block_order, z, xh, y):
    team = jnp.arange(4, dtype=jnp.int32)
    mine = ((z * 2 + xh) * 4 + jnp.arange(4, dtype=jnp.int32))[:, None] * 4 + team[None, :]
    theirs = (jnp.arange(8, dtype=jnp.int32) * 4 + y)[:, None] * 4 + team[None, :]
    qsrc, qpos = in_order(pick(block_order, mine.reshape(-1)))
    ksrc, kpos = in_order(pick(block_order, theirs.reshape(-1)))
    ends = qpos.reshape(NT, QT)
    below = jnp.sum((kpos[None, :] < ends[:, :1]).astype(jnp.int32), axis=1)
    upto = jnp.sum((kpos[None, :] <= ends[:, -1:]).astype(jnp.int32), axis=1)
    return (qsrc, qpos, ksrc, kpos, below // CH, (upto + CH - 1) // CH)


def rotate(x, cosine, sine):
    a, b = x[:, :, : ROT // 2], x[:, :, ROT // 2 : ROT]
    return jnp.concatenate(
        [a * cosine - b * sine, b * cosine + a * sine, x[:, :, ROT:]], axis=2
    )


def dot(a, b, dims):
    return lax.dot_general(a, b, (dims, ((), ())), preferred_element_type=F32)


def local(
    tokens,
    block_order,
    cotangent,
    ln_gain_attn,
    ln_bias_attn,
    ln_gain_mlp,
    ln_bias_mlp,
    w_qkv,
    b_qkv,
    w_out,
    b_out,
    w_fc1,
    b_fc1,
    w_fc2,
    b_fc2,
):
    z, xh, y, core, fsdp = (lax.axis_index(a) for a in AXES)
    team = core * 2 + fsdp
    mine = fsdp * 2 + core
    theirs = (1 - fsdp) * 2 + core
    swap = [(0, 1), (1, 0)]

    def columns(w, which, width):
        return lax.dynamic_slice_in_dim(w, which * width, width, axis=1)

    def qkv_columns(w, which):
        return jnp.concatenate(
            [columns(w[:, i * D : (i + 1) * D], which, HW) for i in range(3)], axis=1
        )

    def whole_rows(keep, send):
        other = lax.ppermute(send, "fsdp", swap)
        return jnp.where(
            fsdp == 0, jnp.concatenate([keep, other]), jnp.concatenate([other, keep])
        )

    x4 = lax.all_gather(tokens, TEAM, axis=0, tiled=True)
    w_q = whole_rows(qkv_columns(w_qkv, mine), qkv_columns(w_qkv, theirs))
    vectors = lax.all_gather(
        jnp.concatenate(
            [ln_gain_attn, ln_bias_attn, ln_gain_mlp, ln_bias_mlp, b_out, b_fc2, b_qkv]
        ),
        "fsdp",
        axis=0,
        tiled=False,
    ).astype(F32)
    g_attn, c_attn, g_mlp, c_mlp, bias_out, bias_two = (
        vectors[:, i * 384 : (i + 1) * 384].reshape(D) for i in range(6)
    )
    bias_qkv = vectors[:, 6 * 384 :].reshape(3, 4, HW)
    bias_qkv = lax.dynamic_index_in_dim(bias_qkv, mine, 1, keepdims=False).reshape(3 * HW)
    dy4 = lax.all_gather(cotangent, TEAM, axis=0, tiled=True)
    w_one = whole_rows(columns(w_fc1, mine, D), columns(w_fc1, theirs, D))
    w_o = lax.dynamic_slice_in_dim(w_out, core * HW, HW, axis=0)
    w_two = lax.dynamic_slice_in_dim(w_fc2, core * D, D, axis=0)
    b_one = lax.dynamic_slice_in_dim(b_fc1, core * D, D, axis=0).astype(F32)

    plan = make_plan(block_order, z, xh, y)

    x = x4.astype(F32)
    centred = x - jnp.mean(x, axis=1, keepdims=True)
    scale = lax.rsqrt(jnp.mean(centred * centred, axis=1, keepdims=True) + EPS)
    n = centred * scale
    a_attn = (n * g_attn + c_attn).astype(BF)
    a_mlp = (n * g_mlp + c_mlp).astype(BF)

    qkv = dot(w_q, a_attn, ((0,), (1,))) + bias_qkv[:, None]
    qkv = qkv.reshape(3, NH, HEAD, TEAM_ROWS)
    group = (z * 2 + xh) * 4 + y
    anchors = pick(block_order, group * 4 + jnp.arange(4, dtype=jnp.int32))
    places = (anchors[:, None] * BLK + jnp.arange(BLK, dtype=jnp.int32)[None, :]).reshape(-1)
    frequency = jnp.exp(jnp.arange(ROT // 2, dtype=F32) * (-2.0 * math.log(10000.0) / ROT))
    angles = frequency[:, None] * places.astype(F32)[None, :]
    cosine, sine = jnp.cos(angles), jnp.sin(angles)
    turned = rotate(qkv[:2], cosine, sine).astype(BF)
    d_mixed = dot(w_o, dy4, ((1,), (1,))).astype(BF).reshape(NH, HEAD, TEAM_ROWS)
    qd = jnp.stack([turned[0] * jnp.asarray(0.125, BF), d_mixed], axis=1)
    kv = jnp.stack([turned[1], qkv[2].astype(BF)], axis=1)
    qd_all = lax.all_gather(qd.reshape(2 * HW, TEAM_ROWS), "y", axis=0, tiled=False)
    kv_all = lax.all_gather(kv.reshape(2 * HW, TEAM_ROWS), KEYS, axis=0, tiled=False)

    hidden_pre = dot(a_mlp, w_one, ((1,), (0,))) + b_one
    hidden_act, gelu_pull = jax.vjp(partial(jax.nn.gelu, approximate=False), hidden_pre)
    act = hidden_act.astype(BF)
    out_part = dot(act, w_two, ((1,), (0,)))
    d_act = dot(dy4, w_two, ((1,), (1,)))
    d_hidden = gelu_pull(d_act)[0].astype(BF)
    grad_one = dot(a_mlp, d_hidden, ((0,), (0,)))
    grad_two = dot(act, dy4, ((0,), (0,)))
    grad_b_one = jnp.sum(d_hidden.astype(F32), axis=0)
    dh_mlp = dot(d_hidden, w_one, ((1,), (1,)))

    def summed(parts):
        took = lax.all_to_all(parts, GROUPS, 0, 0, tiled=True)
        return jnp.sum(took.astype(F32), axis=0)

    first = summed(
        jnp.concatenate(
            [grad_one.astype(BF).reshape(32, 24, D), grad_two.astype(BF).reshape(32, 24, D)], axis=1
        )
    ).astype(BF)

    def to_owner(part):
        pairs = []
        shape = (4, 2)
        for at in range(8):
            zz, f = at // 2, at % 2
            if f == 0 and zz >= 2:
                pairs.append((at, (zz - 2) * 2 + 1))
            elif f == 1 and zz < 2:
                pairs.append((at, (zz + 2) * 2))
            else:
                pairs.append((at, at))
        return lax.ppermute(part, ("z", "fsdp"), pairs)

    first = jnp.concatenate([to_owner(first[:24]), first[24:]], axis=0)
    first_all = lax.all_gather(first, CTX, axis=0, tiled=False)

    partial_out = attend_forward(plan, qd_all, kv_all)
    parts = lax.all_to_all(partial_out, "y", 0, 0, tiled=True).astype(F32)
    o_parts = parts[:, :HW].reshape(4, NH, HEAD, TEAM_ROWS)
    lse_parts = jnp.sum(parts[:, HW : HW + 3 * NH].reshape(4, NH, 3, TEAM_ROWS), axis=2)
    peak = jnp.max(lse_parts, axis=0)
    share = jnp.exp(lse_parts - peak[None])
    total = jnp.sum(share, axis=0)
    attended = jnp.sum(o_parts * (share / total[None])[:, :, None, :], axis=0)
    lse = peak + jnp.log(total)
    delta = jnp.sum(attended * d_mixed.astype(F32), axis=1)
    mixed = attended.astype(BF).reshape(HW, TEAM_ROWS)
    ld = jnp.concatenate([lse, delta, jnp.zeros((2, TEAM_ROWS), F32)], axis=0)
    ld_all = lax.all_gather(ld, "y", axis=0, tiled=False)

    dq_parts, dkv_parts = attend_backward(plan, qd_all, kv_all, ld_all)
    dq = jnp.sum(lax.all_to_all(dq_parts, "y", 0, 0, tiled=True).astype(F32), axis=0)
    dkv = jnp.sum(lax.all_to_all(dkv_parts, KEYS, 0, 0, tiled=True).astype(F32), axis=0)
    dkv = dkv.reshape(NH, 2, HEAD, TEAM_ROWS)
    back = rotate(jnp.stack([dq.reshape(NH, HEAD, TEAM_ROWS), dkv[:, 0]]), cosine, -sine)
    d_qkv = jnp.concatenate([back, dkv[None, :, 1]], axis=0).astype(BF)
    d_qkv = d_qkv.reshape(3 * HW, TEAM_ROWS)

    out_part = out_part + dot(mixed, w_o, ((0,), (0,)))
    grad_qkv = dot(a_attn, d_qkv, ((0,), (1,)))
    grad_out_t = dot(dy4, mixed, ((0,), (1,)))
    second = summed(
        jnp.concatenate([grad_qkv.astype(BF), grad_out_t.astype(BF)], axis=1).reshape(32, 24, D)
    ).astype(BF)
    second = jnp.concatenate([to_owner(second[:, : 3 * HW]), second[:, 3 * HW :]], axis=1)
    second_all = lax.all_gather(second, CTX, axis=0, tiled=False)

    dh_attn = dot(d_qkv, w_q, ((0,), (1,)))
    dn_part = dh_attn * g_attn + dh_mlp * g_mlp
    both = jnp.concatenate([out_part.astype(BF), dn_part.astype(BF)], axis=1)
    both = lax.all_to_all(both.reshape(4, BLK, 2 * D), TEAM, 0, 0, tiled=True)
    both = jnp.sum(both.astype(F32), axis=0)
    own = tokens.astype(F32)
    layer_out = (own + both[:, :D] + bias_out + bias_two).astype(BF)
    own_centred = own - jnp.mean(own, axis=1, keepdims=True)
    own_scale = lax.rsqrt(jnp.mean(own_centred * own_centred, axis=1, keepdims=True) + EPS)
    own_n = own_centred * own_scale
    dn = both[:, D:]
    grad_tokens = cotangent.astype(F32) + own_scale * (
        dn
        - jnp.mean(dn, axis=1, keepdims=True)
        - own_n * jnp.mean(dn * own_n, axis=1, keepdims=True)
    )

    def placed(part, width):
        return jnp.where(
            jnp.arange(4, dtype=jnp.int32)[:, None] == mine, part.reshape(-1, 1, width), 0.0
        ).reshape(-1)

    small = jnp.concatenate(
        [
            jnp.sum(dh_attn * n, axis=0),
            jnp.sum(dh_attn, axis=0),
            jnp.sum(dh_mlp * n, axis=0),
            jnp.sum(dh_mlp, axis=0),
            jnp.sum(cotangent.astype(F32), axis=0),
            placed(jnp.sum(d_qkv.astype(F32), axis=1), HW),
            placed(grad_b_one, D),
        ]
    )
    small = lax.psum(small, AXES)

    def half(start, width):
        return lax.dynamic_slice_in_dim(small, start + fsdp * (width // 2), width // 2)

    first_all = first_all.reshape(2, 16, 2, 2, 24, D)
    second_all = second_all.reshape(2, 16, 2, 24, D)
    grad_w_one = (
        first_all[:, :, :, 0].transpose(1, 3, 0, 2, 4).reshape(384, FF).astype(F32)
    )
    grad_w_two = (
        first_all[:, :, :, 1].transpose(2, 0, 1, 3, 4).reshape(FF // 2, D).astype(F32)
    )
    grad_w_qkv = (
        second_all[..., : 3 * HW]
        .reshape(2, 16, 2, 24, 3, HW)
        .transpose(1, 3, 4, 0, 2, 5)
        .reshape(384, 3 * D)
        .astype(F32)
    )
    grad_w_out = (
        second_all[..., 3 * HW :].transpose(2, 4, 0, 1, 3).reshape(384, D).astype(F32)
    )
    grad_b_out = half(4 * D, D)
    return (
        layer_out,
        grad_tokens,
        half(0, D),
        half(D, D),
        half(2 * D, D),
        half(3 * D, D),
        grad_w_qkv,
        half(5 * D, 3 * D),
        grad_w_out,
        grad_b_out,
        grad_w_one,
        half(8 * D, FF),
        grad_w_two,
        grad_b_out,
    )


def solution(mesh):
    fine = Mesh(mesh.devices.reshape(SIZES), AXES)
    rows = P(AXES, None)
    vec = P("fsdp")
    mat = P("fsdp", None)
    return jax.shard_map(
        local,
        mesh=fine,
        in_specs=(
            rows, P(), rows, vec, vec, vec, vec, mat, vec, mat, vec, mat, vec, mat, vec,
        ),
        out_specs=(
            rows, rows, vec, vec, vec, vec, mat, vec, mat, vec, mat, vec, mat, vec,
        ),
        check_vma=False,
    )
```

```python
from functools import partial
import math

import jax
import jax.numpy as jnp
from jax import lax
from jax.experimental import pallas as pl
from jax.experimental.pallas import tpu as pltpu
from jax.sharding import Mesh, PartitionSpec as P

HEADS = 12
HEAD = 64
ROT = 16
D = 768
FF = 3072
BLK = 128
EPS = 1e-05
MASKED = -1e30
FLOOR = -1e20

AXES = ("z", "xh", "y", "core", "fsdp")
SIZES = (4, 2, 4, 2, 2)
CTX = ("z", "xh", "y", "core")
TEAM = ("core", "fsdp")
KEYS = ("z", "xh")
GROUPS = ("z", "xh", "y")

NH = 3
HW = NH * HEAD
TEAM_ROWS = 512
NQ = 16
NK = 32
QT = 2
CH = 4
NT = NQ // QT
BF = jnp.bfloat16
F32 = jnp.float32
VMEM_LIMIT = 56 * 1024 * 1024


def _sort_keys(kv_ref, ksrc, kvt, kn):
    def step(r, _):
        src = ksrc[r]
        at = pl.multiple_of((src % 4) * BLK, BLK)
        to = pl.multiple_of(r * BLK, BLK)
        blk = kv_ref[src // 4, :, pl.ds(at, BLK)]
        kvt[:, pl.ds(to, BLK)] = blk
        for h in range(NH):
            kn[h, pl.ds(to, BLK), :] = blk[2 * HEAD * h : 2 * HEAD * (h + 1)].T
        return 0

    lax.fori_loop(0, NK, step, 0)


def _tile_columns(ref, qsrc, t, rows):
    parts = []
    for i in range(QT):
        src = qsrc[t * QT + i]
        at = pl.multiple_of((src % 4) * BLK, BLK)
        parts.append(ref[src // 4, rows, pl.ds(at, BLK)])
    return jnp.concatenate(parts, axis=1)


def _allowed(kpos, qpos, t, c):
    row = lax.broadcasted_iota(jnp.int32, (BLK, QT * BLK), 0)
    col = lax.broadcasted_iota(jnp.int32, (BLK, BLK), 1)
    query = jnp.concatenate([qpos[t * QT + i] * BLK + col for i in range(QT)], axis=1)
    return jnp.concatenate([kpos[c * CH + i] * BLK + row <= query for i in range(CH)], axis=0)


def _forward(qsrc, qpos, ksrc, kpos, nfull, nall, qd_ref, kv_ref, o_ref, kvt, kn):
    _sort_keys(kv_ref, ksrc, kvt, kn)
    width = QT * BLK
    rows = CH * BLK

    def tile(t, _):
        blk = _tile_columns(qd_ref, qsrc, t, slice(None))
        half = lax.broadcasted_iota(jnp.int32, (2 * HEAD, width), 0) < HEAD
        zero = jnp.zeros((2 * HEAD, width), BF)
        queries = [
            jnp.where(half, blk[2 * HEAD * h : 2 * HEAD * (h + 1)], zero) for h in range(NH)
        ]

        def chunk(masked, c, carry):
            at = pl.multiple_of(c * rows, rows)
            out = []
            if masked:
                ok = _allowed(kpos, qpos, t, c)
            for h in range(NH):
                m, l, acc = carry[h]
                s = jnp.dot(kn[h, pl.ds(at, rows), :], queries[h], preferred_element_type=F32)
                if masked:
                    s = jnp.where(ok, s, MASKED)
                new = jnp.maximum(m, jnp.max(s, axis=0, keepdims=True))
                p = jnp.exp(s - new)
                fade = jnp.exp(m - new)
                l = l * fade + jnp.sum(p, axis=0, keepdims=True)
                v = kvt[2 * HEAD * h + HEAD : 2 * HEAD * (h + 1), pl.ds(at, rows)]
                acc = acc * fade + jnp.dot(v, p.astype(BF), preferred_element_type=F32)
                out.append((new, l, acc))
            return tuple(out)

        start = tuple(
            (
                jnp.full((1, width), FLOOR, F32),
                jnp.zeros((1, width), F32),
                jnp.zeros((HEAD, width), F32),
            )
            for _ in range(NH)
        )
        state = lax.fori_loop(0, nfull[t], partial(chunk, False), start)
        state = lax.fori_loop(nfull[t], nall[t], partial(chunk, True), state)
        stats = []
        for h in range(NH):
            m, l, acc = state[h]
            some = l > 0.0
            safe = jnp.where(some, l, 1.0)
            o = (acc / safe).astype(BF)
            lse = jnp.where(some, m + jnp.log(safe), FLOOR)
            hi = lse.astype(BF)
            rest = lse - hi.astype(F32)
            mid = rest.astype(BF)
            low = (rest - mid.astype(F32)).astype(BF)
            stats += [hi.astype(F32), mid.astype(F32), low.astype(F32)]
            for i in range(QT):
                src = qsrc[t * QT + i]
                at = pl.multiple_of((src % 4) * BLK, BLK)
                o_ref[src // 4, HEAD * h : HEAD * (h + 1), pl.ds(at, BLK)] = o[:, i * BLK : (i + 1) * BLK]
        stats = jnp.concatenate(stats + [jnp.zeros((16 - 3 * NH, width), F32)], axis=0).astype(BF)
        for i in range(QT):
            src = qsrc[t * QT + i]
            at = pl.multiple_of((src % 4) * BLK, BLK)
            o_ref[src // 4, HW : HW + 16, pl.ds(at, BLK)] = stats[:, i * BLK : (i + 1) * BLK]
        return 0

    lax.fori_loop(0, NT, tile, 0)


def _backward(
    qsrc, qpos, ksrc, kpos, nfull, nall, qd_ref, kv_ref, ld_ref, dq_ref, dkv_ref, kvt, kn, acc, w1, w2, dq
):
    _sort_keys(kv_ref, ksrc, kvt, kn)
    width = QT * BLK
    rows = CH * BLK
    acc[...] = jnp.zeros_like(acc)

    def tile(t, _):
        blk = _tile_columns(qd_ref, qsrc, t, slice(None))
        stats = _tile_columns(ld_ref, qsrc, t, slice(None))
        top = lax.broadcasted_iota(jnp.int32, (2 * HEAD, width), 0) < HEAD
        left = lax.broadcasted_iota(jnp.int32, (width, 2 * HEAD), 1) < HEAD
        zero = jnp.zeros((2 * HEAD, width), BF)
        zero_t = jnp.zeros((width, 2 * HEAD), BF)
        for h in range(NH):
            both = blk[2 * HEAD * h : 2 * HEAD * (h + 1)]
            w1[h, :, :width] = jnp.where(top, both, zero)
            w1[h, :, width:] = jnp.where(top, zero, both)
            turned = both.T
            w2[h, :width, :] = jnp.where(left, turned, zero_t)
            w2[h, width:, :] = jnp.where(left, zero_t, turned)
        dq[...] = jnp.zeros_like(dq)

        def chunk(masked, c, _):
            at = pl.multiple_of(c * rows, rows)
            if masked:
                ok = _allowed(kpos, qpos, t, c)
            for h in range(NH):
                sd = jnp.dot(kn[h, pl.ds(at, rows), :], w1[h], preferred_element_type=F32)
                s = sd[:, :width]
                if masked:
                    s = jnp.where(ok, s, MASKED)
                p = jnp.exp(s - stats[h : h + 1])
                ds = (p * (sd[:, width:] - stats[NH + h : NH + h + 1])).astype(BF)
                pd = jnp.concatenate([ds, p.astype(BF)], axis=1)
                acc[h, pl.ds(at, rows), :] += jnp.dot(pd, w2[h], preferred_element_type=F32)
                k = kvt[2 * HEAD * h : 2 * HEAD * h + HEAD, pl.ds(at, rows)]
                dq[h] += jnp.dot(k, ds, preferred_element_type=F32)
            return 0

        lax.fori_loop(0, nfull[t], partial(chunk, False), 0)
        lax.fori_loop(nfull[t], nall[t], partial(chunk, True), 0)
        for h in range(NH):
            out = (dq[h] * 0.125).astype(BF)
            for i in range(QT):
                src = qsrc[t * QT + i]
                at = pl.multiple_of((src % 4) * BLK, BLK)
                dq_ref[src // 4, HEAD * h : HEAD * (h + 1), pl.ds(at, BLK)] = out[:, i * BLK : (i + 1) * BLK]
        return 0

    lax.fori_loop(0, NT, tile, 0)

    def back(r, _):
        src = ksrc[r]
        at = pl.multiple_of((src % 4) * BLK, BLK)
        for h in range(NH):
            part = acc[h, pl.ds(pl.multiple_of(r * BLK, BLK), BLK), :].T.astype(BF)
            dkv_ref[src // 4, 2 * HEAD * h : 2 * HEAD * (h + 1), pl.ds(at, BLK)] = part
        return 0

    lax.fori_loop(0, NK, back, 0)


def _specs(n):
    return [pl.BlockSpec(memory_space=pltpu.VMEM)] * n


def attend_forward(plan, qd, kv):
    return pl.pallas_call(
        _forward,
        out_shape=jax.ShapeDtypeStruct((4, HW + 16, TEAM_ROWS), BF),
        in_specs=[pl.BlockSpec(memory_space=pltpu.SMEM)] * 6 + _specs(2),
        out_specs=pl.BlockSpec(memory_space=pltpu.VMEM),
        scratch_shapes=[
            pltpu.VMEM((2 * HW, NK * BLK), BF),
            pltpu.VMEM((NH, NK * BLK, 2 * HEAD), BF),
        ],
        compiler_params=pltpu.CompilerParams(vmem_limit_bytes=VMEM_LIMIT),
        name="attend_forward",
    )(*plan, qd, kv)


def attend_backward(plan, qd, kv, ld):
    width = QT * BLK
    return pl.pallas_call(
        _backward,
        out_shape=(
            jax.ShapeDtypeStruct((4, HW, TEAM_ROWS), BF),
            jax.ShapeDtypeStruct((8, 2 * HW, TEAM_ROWS), BF),
        ),
        in_specs=[pl.BlockSpec(memory_space=pltpu.SMEM)] * 6 + _specs(3),
        out_specs=tuple(_specs(2)),
        scratch_shapes=[
            pltpu.VMEM((2 * HW, NK * BLK), BF),
            pltpu.VMEM((NH, NK * BLK, 2 * HEAD), BF),
            pltpu.VMEM((NH, NK * BLK, 2 * HEAD), F32),
            pltpu.VMEM((NH, 2 * HEAD, 2 * width), BF),
            pltpu.VMEM((NH, 2 * width, 2 * HEAD), BF),
            pltpu.VMEM((NH, HEAD, width), F32),
        ],
        compiler_params=pltpu.CompilerParams(vmem_limit_bytes=VMEM_LIMIT),
        name="attend_backward",
    )(*plan, qd, kv, ld)


def pick(table, index):
    ids = jnp.arange(table.shape[0], dtype=jnp.int32)
    return jnp.sum(jnp.where(index[:, None] == ids[None, :], table[None, :], 0), axis=1)


def in_order(pos):
    ids = jnp.arange(pos.shape[0], dtype=jnp.int32)
    rank = jnp.sum((pos[None, :] < pos[:, None]).astype(jnp.int32), axis=1)
    hit = rank[None, :] == ids[:, None]
    return (
        jnp.sum(jnp.where(hit, ids[None, :], 0), axis=1),
        jnp.sum(jnp.where(hit, pos[None, :], 0), axis=1),
    )


def make_plan(block_order, team, z, xh, y):
    rows = jnp.arange(4, dtype=jnp.int32) ^ team
    other = (y + jnp.arange(4, dtype=jnp.int32)) % 4
    mine = ((z * 2 + xh) * 4 + other)[:, None] * 4 + rows[None, :]
    step = jnp.arange(8, dtype=jnp.int32)
    there = ((z + step // 2) % 4) * 2 + (xh ^ (step % 2))
    theirs = (there * 4 + y)[:, None] * 4 + rows[None, :]
    qsrc, qpos = in_order(pick(block_order, mine.reshape(-1)))
    ksrc, kpos = in_order(pick(block_order, theirs.reshape(-1)))
    ends = qpos.reshape(NT, QT)
    below = jnp.sum((kpos[None, :] < ends[:, :1]).astype(jnp.int32), axis=1)
    upto = jnp.sum((kpos[None, :] <= ends[:, -1:]).astype(jnp.int32), axis=1)
    return (qsrc, qpos, ksrc, kpos, below // CH, (upto + CH - 1) // CH)


def from_y(x, i):
    return lax.ppermute(x, "y", [((d + i) % 4, d) for d in range(4)])


def to_y(x, i):
    return lax.ppermute(x, "y", [(d, (d + i) % 4) for d in range(4)])


def _key_pairs(i):
    pairs = []
    for d in range(8):
        there = ((d // 2 + i // 2) % 4) * 2 + ((d % 2) ^ (i % 2))
        pairs.append((d, there))
    return pairs


def from_keys(x, i):
    return lax.ppermute(x, KEYS, [(b, a) for a, b in _key_pairs(i)])


def to_keys(x, i):
    return lax.ppermute(x, KEYS, _key_pairs(i))


def swapped(x, axis):
    return lax.ppermute(x, axis, [(0, 1), (1, 0)])


def team_rows(x):
    pair = jnp.concatenate([x, swapped(x, "fsdp")])
    return jnp.concatenate([pair, swapped(pair, "core")])


def to_all_groups(x):
    sent = jnp.broadcast_to(x[None], (32,) + x.shape)
    took = lax.all_to_all(sent, GROUPS, 0, 0, tiled=True)
    other = swapped(took, "core")
    first = lax.axis_index("core") == 0
    return jnp.where(first, took, other), jnp.where(first, other, took)


def _format_first(a_ref, b_ref, one_ref, two_ref):
    def put(ref):
        for i in range(16):
            block = ref[0, i].astype(F32)
            one_ref[24 * i : 24 * (i + 1), :] = block[:24]
            two_ref[24 * i : 24 * (i + 1), :] = block[24:48]

    @pl.when(pl.program_id(1) == 0)
    def _():
        put(a_ref)

    @pl.when(pl.program_id(1) == 1)
    def _():
        put(b_ref)


def format_first(a, b):
    n = a.shape[1]
    block = pl.BlockSpec((1, 16, n, D), lambda zh, c: (zh, 0, 0, 0))
    return pl.pallas_call(
        _format_first,
        grid=(2, 2),
        out_shape=(
            jax.ShapeDtypeStruct((384, FF), F32),
            jax.ShapeDtypeStruct((FF // 2, D), F32),
        ),
        in_specs=[block, block],
        out_specs=(
            pl.BlockSpec((384, D), lambda zh, c: (0, zh * 2 + c)),
            pl.BlockSpec((384, D), lambda zh, c: (c * 2 + zh, 0)),
        ),
        compiler_params=pltpu.CompilerParams(vmem_limit_bytes=VMEM_LIMIT),
        name="format_first",
    )(a.reshape(2, 16, n, D), b.reshape(2, 16, n, D))


def _format_second(a_ref, b_ref, qkv_ref, out_ref):
    for c, ref in enumerate((a_ref, b_ref)):
        turned = []
        for zh in range(2):
            h = zh * 2 + c
            for i in range(16):
                block = ref[zh * 16 + i].astype(F32)[:24]
                for p in range(3):
                    at = p * D + h * HW
                    qkv_ref[24 * i : 24 * (i + 1), at : at + HW] = block[:, p * HW : (p + 1) * HW]
                turned.append(block[:, 3 * HW :])
        out_ref[c * HW : (c + 1) * HW, :] = jnp.concatenate(turned, axis=0).T


def format_second(a, b):
    return pl.pallas_call(
        _format_second,
        out_shape=(
            jax.ShapeDtypeStruct((384, 3 * D), F32),
            jax.ShapeDtypeStruct((384, D), F32),
        ),
        in_specs=_specs(2),
        out_specs=tuple(_specs(2)),
        compiler_params=pltpu.CompilerParams(vmem_limit_bytes=VMEM_LIMIT),
        name="format_second",
    )(a, b)


def rotate(x, cosine, sine):
    a, b = x[:, :, : ROT // 2], x[:, :, ROT // 2 : ROT]
    return jnp.concatenate(
        [a * cosine - b * sine, b * cosine + a * sine, x[:, :, ROT:]], axis=2
    )


def dot(a, b, dims):
    return lax.dot_general(a, b, (dims, ((), ())), preferred_element_type=F32)


def local(
    tokens,
    block_order,
    cotangent,
    ln_gain_attn,
    ln_bias_attn,
    ln_gain_mlp,
    ln_bias_mlp,
    w_qkv,
    b_qkv,
    w_out,
    b_out,
    w_fc1,
    b_fc1,
    w_fc2,
    b_fc2,
):
    z, xh, y, core, fsdp = (lax.axis_index(a) for a in AXES)
    team = core * 2 + fsdp
    mine = fsdp * 2 + core
    theirs = (1 - fsdp) * 2 + core
    group = (z * 2 + xh) * 4 + y

    def columns(w, which, width):
        return lax.dynamic_slice_in_dim(w, which * width, width, axis=1)

    def qkv_columns(w, which):
        return jnp.concatenate(
            [columns(w[:, i * D : (i + 1) * D], which, HW) for i in range(3)], axis=1
        )

    def ordered(keep, other):
        return (jnp.where(fsdp == 0, keep, other), jnp.where(fsdp == 0, other, keep))

    def whole_rows(keep, send):
        return jnp.concatenate(ordered(keep, swapped(send, "fsdp")))

    x4 = team_rows(tokens)
    w_q = whole_rows(qkv_columns(w_qkv, mine), qkv_columns(w_qkv, theirs))
    dy4 = team_rows(cotangent)
    vectors = jnp.concatenate(
        [ln_gain_attn, ln_bias_attn, ln_gain_mlp, ln_bias_mlp, b_out, b_fc2, b_qkv]
    ).reshape(27, 128)
    vectors = jnp.stack(ordered(vectors, swapped(vectors, "fsdp"))).astype(F32).reshape(2, -1)
    g_attn, c_attn, g_mlp, c_mlp, bias_out, bias_two = (
        vectors[:, i * 384 : (i + 1) * 384].reshape(D) for i in range(6)
    )
    bias_qkv = vectors[:, 6 * 384 :].reshape(3, 4, HW)
    bias_qkv = lax.dynamic_index_in_dim(bias_qkv, mine, 1, keepdims=False).reshape(3 * HW)
    w_one = whole_rows(columns(w_fc1, mine, D), columns(w_fc1, theirs, D))
    w_o = lax.dynamic_slice_in_dim(w_out, core * HW, HW, axis=0)
    w_two = lax.dynamic_slice_in_dim(w_fc2, core * D, D, axis=0)
    b_one = lax.dynamic_slice_in_dim(b_fc1, core * D, D, axis=0).astype(F32)

    plan = make_plan(block_order, team, z, xh, y)

    x = x4.astype(F32)
    centred = x - jnp.mean(x, axis=1, keepdims=True)
    scale = lax.rsqrt(jnp.mean(centred * centred, axis=1, keepdims=True) + EPS)
    n = centred * scale
    a_attn = (n * g_attn + c_attn).astype(BF)
    a_mlp = (n * g_mlp + c_mlp).astype(BF)

    qkv = dot(w_q, a_attn, ((0,), (1,))) + bias_qkv[:, None]
    qkv = qkv.reshape(3, NH, HEAD, TEAM_ROWS)
    anchors = pick(block_order, group * 4 + (jnp.arange(4, dtype=jnp.int32) ^ team))
    places = (anchors[:, None] * BLK + jnp.arange(BLK, dtype=jnp.int32)[None, :]).reshape(-1)
    frequency = jnp.exp(jnp.arange(ROT // 2, dtype=F32) * (-2.0 * math.log(10000.0) / ROT))
    angles = frequency[:, None] * places.astype(F32)[None, :]
    cosine, sine = jnp.cos(angles), jnp.sin(angles)
    turned = rotate(qkv[:2], cosine, sine).astype(BF)
    kv = jnp.stack([turned[1], qkv[2].astype(BF)], axis=1).reshape(2 * HW, TEAM_ROWS)
    kv_all = jnp.stack([kv] + [from_keys(kv, i) for i in range(1, 8)])
    d_mixed = dot(w_o, dy4, ((1,), (1,))).astype(BF).reshape(NH, HEAD, TEAM_ROWS)
    qd = jnp.stack([turned[0] * jnp.asarray(0.125, BF), d_mixed], axis=1)
    qd = qd.reshape(2 * HW, TEAM_ROWS)
    qd_all = jnp.stack([qd] + [from_y(qd, i) for i in range(1, 4)])

    hidden_pre = dot(a_mlp, w_one, ((1,), (0,))) + b_one
    hidden_act, gelu_pull = jax.vjp(partial(jax.nn.gelu, approximate=False), hidden_pre)
    act = hidden_act.astype(BF)
    out_part = dot(act, w_two, ((1,), (0,)))
    d_act = dot(dy4, w_two, ((1,), (1,)))
    d_hidden = gelu_pull(d_act)[0].astype(BF)
    grad_one = dot(a_mlp, d_hidden, ((0,), (0,)))
    grad_two = dot(act, dy4, ((0,), (0,)))
    grad_b_one = jnp.sum(d_hidden.astype(F32), axis=0)
    dh_mlp = dot(d_hidden, w_one, ((1,), (1,)))

    def row(vectors, width):
        return jnp.pad(vectors.reshape(32, 1, width).astype(BF), ((0, 0), (0, 0), (0, D - width)))

    def summed(parts):
        return jnp.sum(lax.all_to_all(parts, GROUPS, 0, 0, tiled=True).astype(F32), axis=0)

    first = jnp.concatenate(
        [
            grad_one.astype(BF).reshape(32, 24, D),
            grad_two.astype(BF).reshape(32, 24, D),
            row(
                jnp.concatenate(
                    [
                        jnp.sum(dh_mlp * n, axis=0),
                        jnp.sum(dh_mlp, axis=0),
                        jnp.sum(cotangent.astype(F32), axis=0),
                        grad_b_one,
                    ]
                ),
                96,
            ),
        ],
        axis=1,
    )
    first, qd_all, kv_all = lax.optimization_barrier((first, qd_all, kv_all))
    first = lax.all_to_all(first, GROUPS, 0, 0, tiled=True)

    def to_owner(part):
        pairs = []
        for at in range(8):
            zz, f = at // 2, at % 2
            if f == 0 and zz >= 2:
                pairs.append((at, (zz - 2) * 2 + 1))
            elif f == 1 and zz < 2:
                pairs.append((at, (zz + 2) * 2))
            else:
                pairs.append((at, at))
        return lax.ppermute(part, ("z", "fsdp"), pairs)

    partial_out = attend_forward(plan, qd_all, kv_all)
    first, partial_out = lax.optimization_barrier((first, partial_out))
    parts = [partial_out[0]] + [to_y(partial_out[i], i) for i in range(1, 4)]
    parts = jnp.stack(parts).astype(F32)
    o_parts = parts[:, :HW].reshape(4, NH, HEAD, TEAM_ROWS)
    lse_parts = jnp.sum(parts[:, HW : HW + 3 * NH].reshape(4, NH, 3, TEAM_ROWS), axis=2)
    peak = jnp.max(lse_parts, axis=0)
    share = jnp.exp(lse_parts - peak[None])
    total = jnp.sum(share, axis=0)
    attended = jnp.sum(o_parts * (share / total[None])[:, :, None, :], axis=0)
    lse = peak + jnp.log(total)
    delta = jnp.sum(attended * d_mixed.astype(F32), axis=1)
    mixed = attended.astype(BF).reshape(HW, TEAM_ROWS)
    ld = jnp.concatenate([lse, delta, jnp.zeros((2, TEAM_ROWS), F32)], axis=0)
    ld_all = jnp.stack([ld] + [from_y(ld, i) for i in range(1, 4)])

    first = jnp.sum(first.astype(F32), axis=0)
    shares = first[48:]
    shares = shares + jnp.where(group < 24, swapped(shares, "fsdp"), 0.0)
    first = jnp.concatenate(
        [to_owner(first[:24].astype(BF)), first[24:48].astype(BF), shares.astype(BF)], axis=0
    )
    first, ld_all = lax.optimization_barrier((first, ld_all))
    sent = jnp.broadcast_to(first[None], (32,) + first.shape)
    first = lax.all_to_all(sent, GROUPS, 0, 0, tiled=True)

    dq_parts, dkv_parts = attend_backward(plan, qd_all, kv_all, ld_all)
    first, dq_parts, dkv_parts = lax.optimization_barrier((first, dq_parts, dkv_parts))
    dkv = [dkv_parts[0]] + [to_keys(dkv_parts[i], i) for i in range(1, 8)]
    dq = [dq_parts[0]] + [to_y(dq_parts[i], i) for i in range(1, 4)]
    other = swapped(first, "core")
    first_a = jnp.where(core == 0, first, other)
    first_b = jnp.where(core == 0, other, first)
    dq = sum(part.astype(F32) for part in dq)
    dkv = sum(part.astype(F32) for part in dkv)
    dkv = dkv.reshape(NH, 2, HEAD, TEAM_ROWS)
    back = rotate(jnp.stack([dq.reshape(NH, HEAD, TEAM_ROWS), dkv[:, 0]]), cosine, -sine)
    d_qkv = jnp.concatenate([back, dkv[None, :, 1]], axis=0).astype(BF)
    d_qkv = d_qkv.reshape(3 * HW, TEAM_ROWS)

    grad_qkv = dot(a_attn, d_qkv, ((0,), (1,)))
    grad_out_t = dot(dy4, mixed, ((0,), (1,)))
    dh_attn = dot(d_qkv, w_q, ((0,), (1,)))
    grad_b_qkv = jnp.sum(d_qkv.astype(F32), axis=1).reshape(3, 1, HW)
    grad_b_qkv = jnp.where(jnp.arange(4, dtype=jnp.int32)[:, None] == mine, grad_b_qkv, 0.0)
    second = jnp.concatenate(
        [
            jnp.concatenate([grad_qkv.astype(BF), grad_out_t.astype(BF)], axis=1).reshape(32, 24, D),
            row(
                jnp.concatenate(
                    [
                        jnp.sum(dh_attn * n, axis=0),
                        jnp.sum(dh_attn, axis=0),
                        grad_b_qkv.reshape(-1),
                    ]
                ),
                120,
            ),
        ],
        axis=1,
    )
    second = summed(second)
    shares = second[24:]
    shares = shares + swapped(shares, "fsdp")
    second = jnp.concatenate(
        [
            jnp.concatenate(
                [to_owner(second[:24, : 3 * HW].astype(BF)), second[:24, 3 * HW :].astype(BF)], axis=1
            ),
            shares.astype(BF),
        ],
        axis=0,
    )
    second_a, second_b = to_all_groups(second)

    out_part = out_part + dot(mixed, w_o, ((0,), (0,)))
    dn_part = dh_attn * g_attn + dh_mlp * g_mlp
    both = jnp.concatenate([out_part, dn_part], axis=1).reshape(4, BLK, 2 * D)
    both = both[:2] + swapped(both[2:].astype(BF), "core").astype(F32)
    both = both[0] + swapped(both[1].astype(BF), "fsdp").astype(F32)
    own = x[:BLK]
    layer_out = (own + both[:, :D] + bias_out + bias_two).astype(BF)
    dn = both[:, D:]
    grad_tokens = cotangent.astype(F32) + scale[:BLK] * (
        dn
        - jnp.mean(dn, axis=1, keepdims=True)
        - n[:BLK] * jnp.mean(dn * n[:BLK], axis=1, keepdims=True)
    )

    grad_w_one, grad_w_two = format_first(first_a, first_b)
    grad_w_qkv, grad_w_out = format_second(second_a, second_b)
    tail_a, tail_b = (t[:, 48, :96].astype(F32) for t in (first_a, first_b))
    early = (tail_a[:24] + tail_b[:24]).reshape(3, D)
    grad_b_one = jnp.concatenate([tail_a[24:].reshape(D), tail_b[24:].reshape(D)])
    late = second_a[:, 24, :120].astype(F32) + second_b[:, 24, :120].astype(F32)
    late = late.reshape(-1)

    def half(vector):
        width = vector.shape[0] // 2
        return lax.dynamic_slice_in_dim(vector, fsdp * width, width)

    grad_b_out = half(early[2])
    return (
        layer_out,
        grad_tokens,
        half(late[:D]),
        half(late[D : 2 * D]),
        half(early[0]),
        half(early[1]),
        grad_w_qkv,
        half(late[2 * D :]),
        grad_w_out,
        grad_b_out,
        grad_w_one,
        grad_b_one,
        grad_w_two,
        grad_b_out,
    )


def solution(mesh):
    fine = Mesh(mesh.devices.reshape(SIZES), AXES)
    rows = P(AXES, None)
    vec = P("fsdp")
    mat = P("fsdp", None)
    return jax.shard_map(
        local,
        mesh=fine,
        in_specs=(
            rows, P(), rows, vec, vec, vec, vec, mat, vec, mat, vec, mat, vec, mat, vec,
        ),
        out_specs=(
            rows, rows, vec, vec, vec, vec, mat, vec, mat, vec, mat, vec, mat, vec,
        ),
        check_vma=False,
    )
```

```python
from functools import partial
import math

import jax
import jax.numpy as jnp
from jax import lax
from jax.experimental import pallas as pl
from jax.experimental.pallas import tpu as pltpu
from jax.sharding import Mesh, PartitionSpec as P

HEADS = 12
HEAD = 64
ROT = 16
D = 768
FF = 3072
BLK = 128
EPS = 1e-05
MASKED = -1e30
FLOOR = -1e20

AXES = ("z", "xh", "y", "core", "fsdp")
SIZES = (4, 2, 4, 2, 2)
CTX = ("z", "xh", "y", "core")
TEAM = ("core", "fsdp")
KEYS = ("z", "xh")
GROUPS = ("z", "xh", "y")

NH = 1
TH = 3
HW = TH * HEAD
KW = NH * HEAD
TEAM_ROWS = 512
NQ = 16
NK = 32
QT = 2
FQT = 4
CH = 4
PAIR = 2
FPAIR = 2
UNROLL = 4
BF = jnp.bfloat16
F32 = jnp.float32
VMEM_LIMIT = 56 * 1024 * 1024


def _sort_keys(kv_ref, ksrc, kvt, kn):
    def step(r, _):
        src = ksrc[r]
        at = pl.multiple_of((src % 4) * BLK, BLK)
        to = pl.multiple_of(r * BLK, BLK)
        blk = kv_ref[src // 4, :, pl.ds(at, BLK)]
        kvt[:, pl.ds(to, BLK)] = blk
        for h in range(NH):
            kn[h, pl.ds(to, BLK), :] = blk[2 * HEAD * h : 2 * HEAD * (h + 1)].T
        return 0

    lax.fori_loop(0, NK, step, 0, unroll=UNROLL)


def _tile_columns(ref, qsrc, t, rows, qt):
    parts = []
    for i in range(qt):
        src = qsrc[t * qt + i]
        at = pl.multiple_of((src % 4) * BLK, BLK)
        parts.append(ref[src // 4, rows, pl.ds(at, BLK)])
    return jnp.concatenate(parts, axis=1)


def _allowed(kpos, qpos, t, c, qt):
    row = lax.broadcasted_iota(jnp.int32, (BLK, qt * BLK), 0)
    col = lax.broadcasted_iota(jnp.int32, (BLK, BLK), 1)
    query = jnp.concatenate([qpos[t * qt + i] * BLK + col for i in range(qt)], axis=1)
    return jnp.concatenate([kpos[c * CH + i] * BLK + row <= query for i in range(CH)], axis=0)


def _forward(qsrc, qpos, ksrc, kpos, nfull, nall, qd_ref, kv_ref, o_ref, kvt, kn):
    _sort_keys(kv_ref, ksrc, kvt, kn)
    width = FQT * BLK

    def tile(t, _):
        blk = _tile_columns(qd_ref, qsrc, t, slice(None), FQT)
        half = lax.broadcasted_iota(jnp.int32, (2 * HEAD, width), 0) < HEAD
        zero = jnp.zeros((2 * HEAD, width), BF)
        queries = [
            jnp.where(half, blk[2 * HEAD * h : 2 * HEAD * (h + 1)], zero) for h in range(NH)
        ]

        def chunk(masked, step, c, carry):
            rows = step * CH * BLK
            at = pl.multiple_of(c * rows, rows)
            out = []
            if masked:
                ok = _allowed(kpos, qpos, t, c, FQT)
            for h in range(NH):
                m, l, acc = carry[h]
                s = jnp.dot(kn[h, pl.ds(at, rows), :], queries[h], preferred_element_type=F32)
                if masked:
                    s = jnp.where(ok, s, MASKED)
                new = jnp.maximum(m, jnp.max(s, axis=0, keepdims=True))
                p = jnp.exp(s - new)
                fade = jnp.exp(m - new)
                l = l * fade + jnp.sum(p, axis=0, keepdims=True)
                v = kvt[2 * HEAD * h + HEAD : 2 * HEAD * (h + 1), pl.ds(at, rows)]
                acc = acc * fade + jnp.dot(v, p.astype(BF), preferred_element_type=F32)
                out.append((new, l, acc))
            return tuple(out)

        start = tuple(
            (
                jnp.full((1, width), FLOOR, F32),
                jnp.zeros((1, width), F32),
                jnp.zeros((HEAD, width), F32),
            )
            for _ in range(NH)
        )
        wide = nfull[t] // FPAIR
        state = lax.fori_loop(0, wide, partial(chunk, False, FPAIR), start)
        state = lax.fori_loop(wide * FPAIR, nfull[t], partial(chunk, False, 1), state)
        state = lax.fori_loop(nfull[t], nall[t], partial(chunk, True, 1), state)
        stats = []
        for h in range(NH):
            m, l, acc = state[h]
            some = l > 0.0
            safe = jnp.where(some, l, 1.0)
            o = (acc / safe).astype(BF)
            lse = jnp.where(some, m + jnp.log(safe), FLOOR)
            hi = lse.astype(BF)
            rest = lse - hi.astype(F32)
            mid = rest.astype(BF)
            low = (rest - mid.astype(F32)).astype(BF)
            stats += [hi.astype(F32), mid.astype(F32), low.astype(F32)]
            for i in range(FQT):
                src = qsrc[t * FQT + i]
                at = pl.multiple_of((src % 4) * BLK, BLK)
                o_ref[src // 4, HEAD * h : HEAD * (h + 1), pl.ds(at, BLK)] = o[:, i * BLK : (i + 1) * BLK]
        stats = jnp.concatenate(stats + [jnp.zeros((16 - 3 * NH, width), F32)], axis=0).astype(BF)
        for i in range(FQT):
            src = qsrc[t * FQT + i]
            at = pl.multiple_of((src % 4) * BLK, BLK)
            o_ref[src // 4, KW : KW + 16, pl.ds(at, BLK)] = stats[:, i * BLK : (i + 1) * BLK]
        return 0

    lax.fori_loop(0, NQ // FQT, tile, 0)


def _backward(
    qsrc, qpos, ksrc, kpos, nfull, nall, qd_ref, kv_ref, ld_ref, dq_ref, dkv_ref, kvt, kn, acc, w1, w2, dq
):
    _sort_keys(kv_ref, ksrc, kvt, kn)
    width = QT * BLK
    acc[...] = jnp.zeros_like(acc)

    def tile(t, _):
        blk = _tile_columns(qd_ref, qsrc, t, slice(None), QT)
        stats = _tile_columns(ld_ref, qsrc, t, slice(None), QT)
        top = lax.broadcasted_iota(jnp.int32, (2 * HEAD, width), 0) < HEAD
        left = lax.broadcasted_iota(jnp.int32, (width, 2 * HEAD), 1) < HEAD
        zero = jnp.zeros((2 * HEAD, width), BF)
        zero_t = jnp.zeros((width, 2 * HEAD), BF)
        for h in range(NH):
            both = blk[2 * HEAD * h : 2 * HEAD * (h + 1)]
            w1[h, :, :width] = jnp.where(top, both, zero)
            w1[h, :, width:] = jnp.where(top, zero, both)
            turned = both.T
            w2[h, :width, :] = jnp.where(left, turned, zero_t)
            w2[h, width:, :] = jnp.where(left, zero_t, turned)
        dq[...] = jnp.zeros_like(dq)

        def chunk(masked, step, c, _):
            rows = step * CH * BLK
            at = pl.multiple_of(c * rows, rows)
            if masked:
                ok = _allowed(kpos, qpos, t, c, QT)
            for h in range(NH):
                sd = jnp.dot(kn[h, pl.ds(at, rows), :], w1[h], preferred_element_type=F32)
                s = sd[:, :width]
                if masked:
                    s = jnp.where(ok, s, MASKED)
                p = jnp.exp(s - stats[h : h + 1])
                ds = (p * (sd[:, width:] - stats[NH + h : NH + h + 1])).astype(BF)
                pd = jnp.concatenate([ds, p.astype(BF)], axis=1)
                acc[h, pl.ds(at, rows), :] += jnp.dot(pd, w2[h], preferred_element_type=F32)
                k = kvt[2 * HEAD * h : 2 * HEAD * h + HEAD, pl.ds(at, rows)]
                dq[h] += jnp.dot(k, ds, preferred_element_type=F32)
            return 0

        wide = nfull[t] // PAIR
        lax.fori_loop(0, wide, partial(chunk, False, PAIR), 0)
        lax.fori_loop(wide * PAIR, nfull[t], partial(chunk, False, 1), 0)
        lax.fori_loop(nfull[t], nall[t], partial(chunk, True, 1), 0)
        for h in range(NH):
            out = (dq[h] * 0.125).astype(BF)
            for i in range(QT):
                src = qsrc[t * QT + i]
                at = pl.multiple_of((src % 4) * BLK, BLK)
                dq_ref[src // 4, HEAD * h : HEAD * (h + 1), pl.ds(at, BLK)] = out[:, i * BLK : (i + 1) * BLK]
        return 0

    lax.fori_loop(0, NQ // QT, tile, 0)

    def back(r, _):
        src = ksrc[r]
        at = pl.multiple_of((src % 4) * BLK, BLK)
        for h in range(NH):
            part = acc[h, pl.ds(pl.multiple_of(r * BLK, BLK), BLK), :].T.astype(BF)
            dkv_ref[src // 4, 2 * HEAD * h : 2 * HEAD * (h + 1), pl.ds(at, BLK)] = part
        return 0

    lax.fori_loop(0, NK, back, 0, unroll=UNROLL)


def _specs(n):
    return [pl.BlockSpec(memory_space=pltpu.VMEM)] * n


def attend_forward(plan, qd, kv):
    return pl.pallas_call(
        _forward,
        out_shape=jax.ShapeDtypeStruct((4, KW + 16, TEAM_ROWS), BF),
        in_specs=[pl.BlockSpec(memory_space=pltpu.SMEM)] * 6 + _specs(2),
        out_specs=pl.BlockSpec(memory_space=pltpu.VMEM),
        scratch_shapes=[
            pltpu.VMEM((2 * KW, NK * BLK), BF),
            pltpu.VMEM((NH, NK * BLK, 2 * HEAD), BF),
        ],
        compiler_params=pltpu.CompilerParams(vmem_limit_bytes=VMEM_LIMIT),
        cost_estimate=pl.CostEstimate(flops=4 * NH * NQ * NK * BLK * BLK * HEAD, bytes_accessed=4 * NH * (NQ + NK) * BLK * BLK, transcendentals=NH * NQ * NK * BLK * BLK),
        name="attend_forward",
    )(*plan, qd, kv)


def attend_backward(plan, qd, kv, ld):
    width = QT * BLK
    return pl.pallas_call(
        _backward,
        out_shape=(
            jax.ShapeDtypeStruct((4, KW, TEAM_ROWS), BF),
            jax.ShapeDtypeStruct((8, 2 * KW, TEAM_ROWS), BF),
        ),
        in_specs=[pl.BlockSpec(memory_space=pltpu.SMEM)] * 6 + _specs(3),
        out_specs=tuple(_specs(2)),
        scratch_shapes=[
            pltpu.VMEM((2 * KW, NK * BLK), BF),
            pltpu.VMEM((NH, NK * BLK, 2 * HEAD), BF),
            pltpu.VMEM((NH, NK * BLK, 2 * HEAD), F32),
            pltpu.VMEM((NH, 2 * HEAD, 2 * width), BF),
            pltpu.VMEM((NH, 2 * width, 2 * HEAD), BF),
            pltpu.VMEM((NH, HEAD, width), F32),
        ],
        compiler_params=pltpu.CompilerParams(vmem_limit_bytes=VMEM_LIMIT),
        cost_estimate=pl.CostEstimate(flops=10 * NH * NQ * NK * BLK * BLK * HEAD, bytes_accessed=8 * NH * (NQ + NK) * BLK * BLK, transcendentals=NH * NQ * NK * BLK * BLK),
        name="attend_backward",
    )(*plan, qd, kv, ld)


def pick(table, index):
    ids = jnp.arange(table.shape[0], dtype=jnp.int32)
    return jnp.sum(jnp.where(index[:, None] == ids[None, :], table[None, :], 0), axis=1)


def in_order(pos):
    ids = jnp.arange(pos.shape[0], dtype=jnp.int32)
    rank = jnp.sum((pos[None, :] < pos[:, None]).astype(jnp.int32), axis=1)
    hit = rank[None, :] == ids[:, None]
    return (
        jnp.sum(jnp.where(hit, ids[None, :], 0), axis=1),
        jnp.sum(jnp.where(hit, pos[None, :], 0), axis=1),
    )


def make_plan(block_order, team, z, xh, y):
    rows = jnp.arange(4, dtype=jnp.int32) ^ team
    other = (y + jnp.arange(4, dtype=jnp.int32)) % 4
    mine = ((z * 2 + xh) * 4 + other)[:, None] * 4 + rows[None, :]
    theirs = (jnp.arange(8, dtype=jnp.int32) * 4 + y)[:, None] * 4 + rows[None, :]
    qsrc, qpos = in_order(pick(block_order, mine.reshape(-1)))
    ksrc, kpos = in_order(pick(block_order, theirs.reshape(-1)))

    def plan(qt):
        ends = qpos.reshape(NQ // qt, qt)
        below = jnp.sum((kpos[None, :] < ends[:, :1]).astype(jnp.int32), axis=1)
        upto = jnp.sum((kpos[None, :] <= ends[:, -1:]).astype(jnp.int32), axis=1)
        return (qsrc, qpos, ksrc, kpos, below // CH, (upto + CH - 1) // CH)

    return plan(FQT), plan(QT)


def from_y(x, i):
    return lax.ppermute(x, "y", [((d + i) % 4, d) for d in range(4)])


def to_y(x, i):
    return lax.ppermute(x, "y", [(d, (d + i) % 4) for d in range(4)])


def from_keys(x):
    return lax.all_to_all(jnp.broadcast_to(x[None], (8,) + x.shape), KEYS, 0, 0, tiled=True)


def to_keys(parts):
    return lax.all_to_all(parts, KEYS, 0, 0, tiled=True)


def after(values, *done):
    return lax.optimization_barrier((values, done))[0]


def swapped(x, axis):
    return lax.ppermute(x, axis, [(0, 1), (1, 0)])


def team_rows(x):
    pair = jnp.concatenate([x, swapped(x, "fsdp")])
    return jnp.concatenate([pair, swapped(pair, "core")])


def to_all_groups(x):
    sent = jnp.broadcast_to(x[None], (32,) + x.shape)
    took = lax.all_to_all(sent, GROUPS, 0, 0, tiled=True)
    other = swapped(took, "core")
    first = lax.axis_index("core") == 0
    return jnp.where(first, took, other), jnp.where(first, other, took)


def _format_first(all_ref, one_ref, two_ref):
    for i in range(16):
        block = all_ref[0, i, 0].astype(F32)
        one_ref[24 * i : 24 * (i + 1), :] = block[:24]
        two_ref[24 * i : 24 * (i + 1), :] = block[24:48]


def format_first(gathered):
    n = gathered.shape[1]
    return pl.pallas_call(
        _format_first,
        grid=(2, 2),
        out_shape=(
            jax.ShapeDtypeStruct((384, FF), F32),
            jax.ShapeDtypeStruct((FF // 2, D), F32),
        ),
        in_specs=[pl.BlockSpec((1, 16, 1, n, D), lambda zh, c: (zh, 0, c, 0, 0))],
        out_specs=(
            pl.BlockSpec((384, D), lambda zh, c: (0, zh * 2 + c)),
            pl.BlockSpec((384, D), lambda zh, c: (c * 2 + zh, 0)),
        ),
        compiler_params=pltpu.CompilerParams(vmem_limit_bytes=VMEM_LIMIT),
        name="format_first",
    )(gathered.reshape(2, 16, 2, n, D))


def _format_second(a_ref, b_ref, qkv_ref, out_ref):
    for c, ref in enumerate((a_ref, b_ref)):
        turned = []
        for zh in range(2):
            h = zh * 2 + c
            for i in range(16):
                block = ref[zh * 16 + i].astype(F32)[:24]
                for p in range(3):
                    at = p * D + h * HW
                    qkv_ref[24 * i : 24 * (i + 1), at : at + HW] = block[:, p * HW : (p + 1) * HW]
                turned.append(block[:, 3 * HW :])
        out_ref[c * HW : (c + 1) * HW, :] = jnp.concatenate(turned, axis=0).T


def format_second(a, b):
    return pl.pallas_call(
        _format_second,
        out_shape=(
            jax.ShapeDtypeStruct((384, 3 * D), F32),
            jax.ShapeDtypeStruct((384, D), F32),
        ),
        in_specs=_specs(2),
        out_specs=tuple(_specs(2)),
        compiler_params=pltpu.CompilerParams(vmem_limit_bytes=VMEM_LIMIT),
        name="format_second",
    )(a, b)


def rotate(x, cosine, sine):
    a, b = x[:, :, : ROT // 2], x[:, :, ROT // 2 : ROT]
    return jnp.concatenate(
        [a * cosine - b * sine, b * cosine + a * sine, x[:, :, ROT:]], axis=2
    )


def dot(a, b, dims):
    return lax.dot_general(a, b, (dims, ((), ())), preferred_element_type=F32)


def local(
    tokens,
    block_order,
    cotangent,
    ln_gain_attn,
    ln_bias_attn,
    ln_gain_mlp,
    ln_bias_mlp,
    w_qkv,
    b_qkv,
    w_out,
    b_out,
    w_fc1,
    b_fc1,
    w_fc2,
    b_fc2,
):
    z, xh, y, core, fsdp = (lax.axis_index(a) for a in AXES)
    team = core * 2 + fsdp
    mine = fsdp * 2 + core
    theirs = (1 - fsdp) * 2 + core
    group = (z * 2 + xh) * 4 + y

    def columns(w, which, width):
        return lax.dynamic_slice_in_dim(w, which * width, width, axis=1)

    def qkv_columns(w, which):
        return jnp.concatenate(
            [columns(w[:, i * D : (i + 1) * D], which, HW) for i in range(3)], axis=1
        )

    def ordered(keep, other):
        return (jnp.where(fsdp == 0, keep, other), jnp.where(fsdp == 0, other, keep))

    def whole_rows(keep, send):
        return jnp.concatenate(ordered(keep, swapped(send, "fsdp")))

    x4 = team_rows(tokens)
    w_q = whole_rows(qkv_columns(w_qkv, mine), qkv_columns(w_qkv, theirs))
    dy4 = team_rows(cotangent)
    vectors = jnp.concatenate(
        [ln_gain_attn, ln_bias_attn, ln_gain_mlp, ln_bias_mlp, b_out, b_fc2, b_qkv]
    ).reshape(27, 128)
    vectors = jnp.stack(ordered(vectors, swapped(vectors, "fsdp"))).astype(F32).reshape(2, -1)
    g_attn, c_attn, g_mlp, c_mlp, bias_out, bias_two = (
        vectors[:, i * 384 : (i + 1) * 384].reshape(D) for i in range(6)
    )
    bias_qkv = vectors[:, 6 * 384 :].reshape(3, 4, HW)
    bias_qkv = lax.dynamic_index_in_dim(bias_qkv, mine, 1, keepdims=False).reshape(3 * HW)
    w_one = whole_rows(columns(w_fc1, mine, D), columns(w_fc1, theirs, D))
    w_o = lax.dynamic_slice_in_dim(w_out, core * HW, HW, axis=0)
    w_two = lax.dynamic_slice_in_dim(w_fc2, core * D, D, axis=0)
    b_one = lax.dynamic_slice_in_dim(b_fc1, core * D, D, axis=0).astype(F32)

    fplan, bplan = make_plan(block_order, team, z, xh, y)

    x = x4.astype(F32)
    centred = x - jnp.mean(x, axis=1, keepdims=True)
    scale = lax.rsqrt(jnp.mean(centred * centred, axis=1, keepdims=True) + EPS)
    n = centred * scale
    a_attn = (n * g_attn + c_attn).astype(BF)
    a_mlp = (n * g_mlp + c_mlp).astype(BF)

    qkv = dot(w_q, a_attn, ((0,), (1,))) + bias_qkv[:, None]
    qkv = qkv.reshape(3, TH, HEAD, TEAM_ROWS)
    anchors = pick(block_order, group * 4 + (jnp.arange(4, dtype=jnp.int32) ^ team))
    places = (anchors[:, None] * BLK + jnp.arange(BLK, dtype=jnp.int32)[None, :]).reshape(-1)
    frequency = jnp.exp(jnp.arange(ROT // 2, dtype=F32) * (-2.0 * math.log(10000.0) / ROT))
    angles = frequency[:, None] * places.astype(F32)[None, :]
    cosine, sine = jnp.cos(angles), jnp.sin(angles)
    turned = rotate(qkv[:2], cosine, sine).astype(BF)
    values = qkv[2].astype(BF)
    d_mixed = dot(w_o, dy4, ((1,), (1,))).astype(BF).reshape(TH, HEAD, TEAM_ROWS)
    kv_all, qd_all = [], []
    for h in range(TH):
        kv = jnp.concatenate([turned[1, h], values[h]], axis=0)
        qd = jnp.concatenate([turned[0, h] * jnp.asarray(0.125, BF), d_mixed[h]], axis=0)
        kv_all.append(from_keys(kv))
        qd_all.append(jnp.stack([qd] + [from_y(qd, i) for i in range(1, 4)]))

    hidden_pre = dot(a_mlp, w_one, ((1,), (0,))) + b_one
    hidden_act, gelu_pull = jax.vjp(partial(jax.nn.gelu, approximate=False), hidden_pre)
    act = hidden_act.astype(BF)
    out_part = dot(act, w_two, ((1,), (0,)))
    d_act = dot(dy4, w_two, ((1,), (1,)))
    d_hidden = gelu_pull(d_act)[0].astype(BF)
    grad_one = dot(a_mlp, d_hidden, ((0,), (0,)))
    grad_two = dot(act, dy4, ((0,), (0,)))
    grad_b_one = jnp.sum(d_hidden.astype(F32), axis=0)
    dh_mlp = dot(d_hidden, w_one, ((1,), (1,)))

    def row(vectors, width):
        return jnp.pad(vectors.reshape(32, 1, width).astype(BF), ((0, 0), (0, 0), (0, D - width)))

    def summed(parts):
        return jnp.sum(lax.all_to_all(parts, GROUPS, 0, 0, tiled=True).astype(F32), axis=0)

    first = jnp.concatenate(
        [
            grad_one.astype(BF).reshape(32, 24, D),
            grad_two.astype(BF).reshape(32, 24, D),
            row(
                jnp.concatenate(
                    [
                        jnp.sum(dh_mlp * n, axis=0),
                        jnp.sum(dh_mlp, axis=0),
                        jnp.sum(cotangent.astype(F32), axis=0),
                        grad_b_one,
                    ]
                ),
                96,
            ),
        ],
        axis=1,
    )

    def to_owner(part):
        pairs = []
        for at in range(8):
            zz, f = at // 2, at % 2
            if f == 0 and zz >= 2:
                pairs.append((at, (zz - 2) * 2 + 1))
            elif f == 1 and zz < 2:
                pairs.append((at, (zz + 2) * 2))
            else:
                pairs.append((at, at))
        return lax.ppermute(part, ("z", "fsdp"), pairs)

    def merged(out, h, *done):
        parts = after([out[0]] + [to_y(out[i], i) for i in range(1, 4)], *done)
        parts = jnp.stack(parts).astype(F32)
        lse_parts = jnp.sum(parts[:, HEAD : HEAD + 3], axis=1)
        peak = jnp.max(lse_parts, axis=0)
        share = jnp.exp(lse_parts - peak[None])
        total = jnp.sum(share, axis=0)
        whole = jnp.sum(parts[:, :HEAD] * (share / total[None])[:, None, :], axis=0)
        delta = jnp.sum(whole * d_mixed[h].astype(F32), axis=0)
        return whole, jnp.stack([peak + jnp.log(total), delta] + [jnp.zeros_like(delta)] * 6)

    def stats(ld, *done):
        return jnp.stack(after([ld] + [from_y(ld, i) for i in range(1, 4)], *done))

    def pulled(dq_parts, dkv_parts, *done):
        dkv = to_keys(dkv_parts)
        dq = [dq_parts[0]] + [to_y(dq_parts[i], i) for i in range(1, 4)]
        dkv, dq = after((dkv, dq), *done)
        return sum(part.astype(F32) for part in dq), jnp.sum(dkv.astype(F32), axis=0)

    out_0 = attend_forward(fplan, qd_all[0], kv_all[0])
    out_1 = attend_forward(after(fplan, out_0), qd_all[1], kv_all[1])
    first = lax.all_to_all(after(first, out_1), GROUPS, 0, 0, tiled=True)
    whole_0, ld_0 = merged(out_0, 0, out_1)
    out_2 = attend_forward(after(fplan, out_1, ld_0), qd_all[2], kv_all[2])
    ld_0 = stats(ld_0, out_2)
    whole_1, ld_1 = merged(out_1, 1, out_2)
    raw_0 = attend_backward(after(bplan, out_2, ld_1), qd_all[0], kv_all[0], ld_0)
    ld_1 = stats(ld_1, raw_0)
    whole_2, ld_2 = merged(out_2, 2, raw_0)
    first = jnp.sum(after(first, raw_0).astype(F32), axis=0)
    raw_1 = attend_backward(after(bplan, raw_0, ld_2, first), qd_all[1], kv_all[1], ld_1)
    ld_2 = stats(ld_2, raw_1)
    grads_0 = pulled(*raw_0, raw_1)
    raw_2 = attend_backward(after(bplan, raw_1, grads_0), qd_all[2], kv_all[2], ld_2)
    grads_1 = pulled(*raw_1, raw_2)
    grads_2 = pulled(*raw_2)
    mixed = jnp.concatenate([whole_0, whole_1, whole_2]).astype(BF)

    shares = first[48:]
    shares = shares + jnp.where(group < 24, swapped(shares, "fsdp"), 0.0)
    first = jnp.concatenate(
        [to_owner(first[:24].astype(BF)), first[24:48].astype(BF), shares.astype(BF)], axis=0
    )
    first_all = lax.all_gather(first, CTX, axis=0, tiled=False)

    dqs, dks, dvs = [], [], []
    for dq, dkv in (grads_0, grads_1, grads_2):
        dqs.append(dq)
        dks.append(dkv[:HEAD])
        dvs.append(dkv[HEAD:])
    back = rotate(jnp.stack([jnp.stack(dqs), jnp.stack(dks)]), cosine, -sine)
    d_qkv = jnp.concatenate([back, jnp.stack(dvs)[None]], axis=0).astype(BF)
    d_qkv = d_qkv.reshape(3 * HW, TEAM_ROWS)

    grad_qkv = dot(a_attn, d_qkv, ((0,), (1,)))
    grad_out_t = dot(dy4, mixed, ((0,), (1,)))
    dh_attn = dot(d_qkv, w_q, ((0,), (1,)))
    grad_b_qkv = jnp.sum(d_qkv.astype(F32), axis=1).reshape(3, 1, HW)
    grad_b_qkv = jnp.where(jnp.arange(4, dtype=jnp.int32)[:, None] == mine, grad_b_qkv, 0.0)
    second = jnp.concatenate(
        [
            jnp.concatenate([grad_qkv.astype(BF), grad_out_t.astype(BF)], axis=1).reshape(32, 24, D),
            row(
                jnp.concatenate(
                    [
                        jnp.sum(dh_attn * n, axis=0),
                        jnp.sum(dh_attn, axis=0),
                        grad_b_qkv.reshape(-1),
                    ]
                ),
                120,
            ),
        ],
        axis=1,
    )
    second = summed(second)
    shares = second[24:]
    shares = shares + swapped(shares, "fsdp")
    second = jnp.concatenate(
        [
            jnp.concatenate(
                [to_owner(second[:24, : 3 * HW].astype(BF)), second[:24, 3 * HW :].astype(BF)], axis=1
            ),
            shares.astype(BF),
        ],
        axis=0,
    )
    second_a, second_b = to_all_groups(second)

    out_part = out_part + dot(mixed, w_o, ((0,), (0,)))
    dn_part = dh_attn * g_attn + dh_mlp * g_mlp
    both = jnp.concatenate([out_part, dn_part], axis=1).reshape(4, BLK, 2 * D)
    both = both[:2] + swapped(both[2:].astype(BF), "core").astype(F32)
    both = both[0] + swapped(both[1].astype(BF), "fsdp").astype(F32)
    own = x[:BLK]
    layer_out = (own + both[:, :D] + bias_out + bias_two).astype(BF)
    dn = both[:, D:]
    grad_tokens = cotangent.astype(F32) + scale[:BLK] * (
        dn
        - jnp.mean(dn, axis=1, keepdims=True)
        - n[:BLK] * jnp.mean(dn * n[:BLK], axis=1, keepdims=True)
    )

    grad_w_one, grad_w_two = format_first(first_all)
    grad_w_qkv, grad_w_out = format_second(second_a, second_b)
    tails = first_all.reshape(32, 2, -1, D)[:, :, 48, :96].astype(F32)
    tail_a, tail_b = tails[:, 0], tails[:, 1]
    early = (tail_a[:24] + tail_b[:24]).reshape(3, D)
    grad_b_one = jnp.concatenate([tail_a[24:].reshape(D), tail_b[24:].reshape(D)])
    late = second_a[:, 24, :120].astype(F32) + second_b[:, 24, :120].astype(F32)
    late = late.reshape(-1)

    def half(vector):
        width = vector.shape[0] // 2
        return lax.dynamic_slice_in_dim(vector, fsdp * width, width)

    grad_b_out = half(early[2])
    return (
        layer_out,
        grad_tokens,
        half(late[:D]),
        half(late[D : 2 * D]),
        half(early[0]),
        half(early[1]),
        grad_w_qkv,
        half(late[2 * D :]),
        grad_w_out,
        grad_b_out,
        grad_w_one,
        grad_b_one,
        grad_w_two,
        grad_b_out,
    )


def solution(mesh):
    fine = Mesh(mesh.devices.reshape(SIZES), AXES)
    rows = P(AXES, None)
    vec = P("fsdp")
    mat = P("fsdp", None)
    return jax.shard_map(
        local,
        mesh=fine,
        in_specs=(
            rows, P(), rows, vec, vec, vec, vec, mat, vec, mat, vec, mat, vec, mat, vec,
        ),
        out_specs=(
            rows, rows, vec, vec, vec, vec, mat, vec, mat, vec, mat, vec, mat, vec,
        ),
        check_vma=False,
    )
```

```python
from functools import partial
import math

import jax
import jax.numpy as jnp
from jax import lax
from jax.experimental import pallas as pl
from jax.experimental.pallas import tpu as pltpu
from jax.sharding import Mesh, PartitionSpec as P

HEADS = 12
HEAD = 64
ROT = 16
D = 768
FF = 3072
BLK = 128
EPS = 1e-05
MASKED = -1e30
FLOOR = -1e20

AXES = ("z", "xh", "y", "core", "fsdp")
SIZES = (4, 2, 4, 2, 2)
CTX = ("z", "xh", "y", "core")
TEAM = ("core", "fsdp")
KEYS = ("z", "xh")
GROUPS = ("z", "xh", "y")

NH = 1
TH = 3
HW = TH * HEAD
KW = NH * HEAD
TEAM_ROWS = 512
NQ = 16
NK = 32
QT = 2
FQT = 4
CH = 4
PAIR = 2
FPAIR = 2
UNROLL = 4
BF = jnp.bfloat16
F32 = jnp.float32
VMEM_LIMIT = 56 * 1024 * 1024


def _sort_keys(kv_ref, ksrc, kvt, kn):
    def step(r, _):
        src = ksrc[r]
        at = pl.multiple_of((src % 4) * BLK, BLK)
        to = pl.multiple_of(r * BLK, BLK)
        blk = kv_ref[src // 4, :, pl.ds(at, BLK)]
        kvt[:, pl.ds(to, BLK)] = blk
        for h in range(NH):
            kn[h, pl.ds(to, BLK), :] = blk[2 * HEAD * h : 2 * HEAD * (h + 1)].T
        return 0

    lax.fori_loop(0, NK, step, 0, unroll=UNROLL)


def _tile_columns(ref, qsrc, t, rows, qt):
    parts = []
    for i in range(qt):
        src = qsrc[t * qt + i]
        at = pl.multiple_of((src % 4) * BLK, BLK)
        parts.append(ref[src // 4, rows, pl.ds(at, BLK)])
    return jnp.concatenate(parts, axis=1)


def _allowed(kpos, qpos, t, c, qt):
    row = lax.broadcasted_iota(jnp.int32, (BLK, qt * BLK), 0)
    col = lax.broadcasted_iota(jnp.int32, (BLK, BLK), 1)
    query = jnp.concatenate([qpos[t * qt + i] * BLK + col for i in range(qt)], axis=1)
    return jnp.concatenate([kpos[c * CH + i] * BLK + row <= query for i in range(CH)], axis=0)


def _forward(qsrc, qpos, ksrc, kpos, nfull, nall, qd_ref, kv_ref, o_ref, kvt, kn):
    _sort_keys(kv_ref, ksrc, kvt, kn)
    width = FQT * BLK

    def tile(t, _):
        blk = _tile_columns(qd_ref, qsrc, t, slice(None), FQT)
        half = lax.broadcasted_iota(jnp.int32, (2 * HEAD, width), 0) < HEAD
        zero = jnp.zeros((2 * HEAD, width), BF)
        queries = [
            jnp.where(half, blk[2 * HEAD * h : 2 * HEAD * (h + 1)], zero) for h in range(NH)
        ]

        def chunk(masked, step, c, carry):
            rows = step * CH * BLK
            at = pl.multiple_of(c * rows, rows)
            out = []
            if masked:
                ok = _allowed(kpos, qpos, t, c, FQT)
            for h in range(NH):
                m, l, acc = carry[h]
                s = jnp.dot(kn[h, pl.ds(at, rows), :], queries[h], preferred_element_type=F32)
                if masked:
                    s = jnp.where(ok, s, MASKED)
                new = jnp.maximum(m, jnp.max(s, axis=0, keepdims=True))
                p = jnp.exp(s - new)
                fade = jnp.exp(m - new)
                l = l * fade + jnp.sum(p, axis=0, keepdims=True)
                v = kvt[2 * HEAD * h + HEAD : 2 * HEAD * (h + 1), pl.ds(at, rows)]
                acc = acc * fade + jnp.dot(v, p.astype(BF), preferred_element_type=F32)
                out.append((new, l, acc))
            return tuple(out)

        start = tuple(
            (
                jnp.full((1, width), FLOOR, F32),
                jnp.zeros((1, width), F32),
                jnp.zeros((HEAD, width), F32),
            )
            for _ in range(NH)
        )
        wide = nfull[t] // FPAIR
        state = lax.fori_loop(0, wide, partial(chunk, False, FPAIR), start)
        state = lax.fori_loop(wide * FPAIR, nfull[t], partial(chunk, False, 1), state)
        state = lax.fori_loop(nfull[t], nall[t], partial(chunk, True, 1), state)
        stats = []
        for h in range(NH):
            m, l, acc = state[h]
            some = l > 0.0
            safe = jnp.where(some, l, 1.0)
            o = (acc / safe).astype(BF)
            lse = jnp.where(some, m + jnp.log(safe), FLOOR)
            hi = lse.astype(BF)
            rest = lse - hi.astype(F32)
            mid = rest.astype(BF)
            low = (rest - mid.astype(F32)).astype(BF)
            stats += [hi.astype(F32), mid.astype(F32), low.astype(F32)]
            for i in range(FQT):
                src = qsrc[t * FQT + i]
                at = pl.multiple_of((src % 4) * BLK, BLK)
                o_ref[src // 4, HEAD * h : HEAD * (h + 1), pl.ds(at, BLK)] = o[:, i * BLK : (i + 1) * BLK]
        stats = jnp.concatenate(stats + [jnp.zeros((16 - 3 * NH, width), F32)], axis=0).astype(BF)
        for i in range(FQT):
            src = qsrc[t * FQT + i]
            at = pl.multiple_of((src % 4) * BLK, BLK)
            o_ref[src // 4, KW : KW + 16, pl.ds(at, BLK)] = stats[:, i * BLK : (i + 1) * BLK]
        return 0

    lax.fori_loop(0, NQ // FQT, tile, 0)


def _backward(
    qsrc, qpos, ksrc, kpos, nfull, nall, qd_ref, kv_ref, ld_ref, dq_ref, dkv_ref, kvt, kn, acc, w1, w2, dq
):
    _sort_keys(kv_ref, ksrc, kvt, kn)
    width = QT * BLK
    acc[...] = jnp.zeros_like(acc)

    def tile(t, _):
        blk = _tile_columns(qd_ref, qsrc, t, slice(None), QT)
        stats = _tile_columns(ld_ref, qsrc, t, slice(None), QT)
        top = lax.broadcasted_iota(jnp.int32, (2 * HEAD, width), 0) < HEAD
        left = lax.broadcasted_iota(jnp.int32, (width, 2 * HEAD), 1) < HEAD
        zero = jnp.zeros((2 * HEAD, width), BF)
        zero_t = jnp.zeros((width, 2 * HEAD), BF)
        for h in range(NH):
            both = blk[2 * HEAD * h : 2 * HEAD * (h + 1)]
            w1[h, :, :width] = jnp.where(top, both, zero)
            w1[h, :, width:] = jnp.where(top, zero, both)
            turned = both.T
            w2[h, :width, :] = jnp.where(left, turned, zero_t)
            w2[h, width:, :] = jnp.where(left, zero_t, turned)
        dq[...] = jnp.zeros_like(dq)

        def chunk(masked, step, c, _):
            rows = step * CH * BLK
            at = pl.multiple_of(c * rows, rows)
            if masked:
                ok = _allowed(kpos, qpos, t, c, QT)
            for h in range(NH):
                sd = jnp.dot(kn[h, pl.ds(at, rows), :], w1[h], preferred_element_type=F32)
                s = sd[:, :width]
                if masked:
                    s = jnp.where(ok, s, MASKED)
                p = jnp.exp(s - stats[h : h + 1])
                ds = (p * (sd[:, width:] - stats[NH + h : NH + h + 1])).astype(BF)
                pd = jnp.concatenate([ds, p.astype(BF)], axis=1)
                acc[h, pl.ds(at, rows), :] += jnp.dot(pd, w2[h], preferred_element_type=F32)
                k = kvt[2 * HEAD * h : 2 * HEAD * h + HEAD, pl.ds(at, rows)]
                dq[h] += jnp.dot(k, ds, preferred_element_type=F32)
            return 0

        wide = nfull[t] // PAIR
        lax.fori_loop(0, wide, partial(chunk, False, PAIR), 0)
        lax.fori_loop(wide * PAIR, nfull[t], partial(chunk, False, 1), 0)
        lax.fori_loop(nfull[t], nall[t], partial(chunk, True, 1), 0)
        for h in range(NH):
            out = (dq[h] * 0.125).astype(BF)
            for i in range(QT):
                src = qsrc[t * QT + i]
                at = pl.multiple_of((src % 4) * BLK, BLK)
                dq_ref[src // 4, HEAD * h : HEAD * (h + 1), pl.ds(at, BLK)] = out[:, i * BLK : (i + 1) * BLK]
        return 0

    lax.fori_loop(0, NQ // QT, tile, 0)

    def back(r, _):
        src = ksrc[r]
        at = pl.multiple_of((src % 4) * BLK, BLK)
        for h in range(NH):
            part = acc[h, pl.ds(pl.multiple_of(r * BLK, BLK), BLK), :].T.astype(BF)
            dkv_ref[src // 4, 2 * HEAD * h : 2 * HEAD * (h + 1), pl.ds(at, BLK)] = part
        return 0

    lax.fori_loop(0, NK, back, 0, unroll=UNROLL)


def _specs(n):
    return [pl.BlockSpec(memory_space=pltpu.VMEM)] * n


def attend_forward(plan, qd, kv):
    return pl.pallas_call(
        _forward,
        out_shape=jax.ShapeDtypeStruct((4, KW + 16, TEAM_ROWS), BF),
        in_specs=[pl.BlockSpec(memory_space=pltpu.SMEM)] * 6 + _specs(2),
        out_specs=pl.BlockSpec(memory_space=pltpu.VMEM),
        scratch_shapes=[
            pltpu.VMEM((2 * KW, NK * BLK), BF),
            pltpu.VMEM((NH, NK * BLK, 2 * HEAD), BF),
        ],
        compiler_params=pltpu.CompilerParams(vmem_limit_bytes=VMEM_LIMIT),
        cost_estimate=pl.CostEstimate(flops=4 * NH * NQ * NK * BLK * BLK * HEAD, bytes_accessed=4 * NH * (NQ + NK) * BLK * BLK, transcendentals=NH * NQ * NK * BLK * BLK),
        name="attend_forward",
    )(*plan, qd, kv)


def attend_backward(plan, qd, kv, ld):
    width = QT * BLK
    return pl.pallas_call(
        _backward,
        out_shape=(
            jax.ShapeDtypeStruct((4, KW, TEAM_ROWS), BF),
            jax.ShapeDtypeStruct((8, 2 * KW, TEAM_ROWS), BF),
        ),
        in_specs=[pl.BlockSpec(memory_space=pltpu.SMEM)] * 6 + _specs(3),
        out_specs=tuple(_specs(2)),
        scratch_shapes=[
            pltpu.VMEM((2 * KW, NK * BLK), BF),
            pltpu.VMEM((NH, NK * BLK, 2 * HEAD), BF),
            pltpu.VMEM((NH, NK * BLK, 2 * HEAD), F32),
            pltpu.VMEM((NH, 2 * HEAD, 2 * width), BF),
            pltpu.VMEM((NH, 2 * width, 2 * HEAD), BF),
            pltpu.VMEM((NH, HEAD, width), F32),
        ],
        compiler_params=pltpu.CompilerParams(vmem_limit_bytes=VMEM_LIMIT),
        cost_estimate=pl.CostEstimate(flops=10 * NH * NQ * NK * BLK * BLK * HEAD, bytes_accessed=8 * NH * (NQ + NK) * BLK * BLK, transcendentals=NH * NQ * NK * BLK * BLK),
        name="attend_backward",
    )(*plan, qd, kv, ld)


def pick(table, index):
    ids = jnp.arange(table.shape[0], dtype=jnp.int32)
    return jnp.sum(jnp.where(index[:, None] == ids[None, :], table[None, :], 0), axis=1)


def in_order(pos):
    ids = jnp.arange(pos.shape[0], dtype=jnp.int32)
    rank = jnp.sum((pos[None, :] < pos[:, None]).astype(jnp.int32), axis=1)
    hit = rank[None, :] == ids[:, None]
    return (
        jnp.sum(jnp.where(hit, ids[None, :], 0), axis=1),
        jnp.sum(jnp.where(hit, pos[None, :], 0), axis=1),
    )


def make_plan(block_order, team, z, xh, y):
    rows = jnp.arange(4, dtype=jnp.int32) ^ team
    other = (y + jnp.arange(4, dtype=jnp.int32)) % 4
    mine = ((z * 2 + xh) * 4 + other)[:, None] * 4 + rows[None, :]
    theirs = (jnp.arange(8, dtype=jnp.int32) * 4 + y)[:, None] * 4 + rows[None, :]
    qsrc, qpos = in_order(pick(block_order, mine.reshape(-1)))
    ksrc, kpos = in_order(pick(block_order, theirs.reshape(-1)))

    def plan(qt):
        ends = qpos.reshape(NQ // qt, qt)
        below = jnp.sum((kpos[None, :] < ends[:, :1]).astype(jnp.int32), axis=1)
        upto = jnp.sum((kpos[None, :] <= ends[:, -1:]).astype(jnp.int32), axis=1)
        return (qsrc, qpos, ksrc, kpos, below // CH, (upto + CH - 1) // CH)

    return plan(FQT), plan(QT)


def from_y(x, i):
    return lax.ppermute(x, "y", [((d + i) % 4, d) for d in range(4)])


def to_y(x, i):
    return lax.ppermute(x, "y", [(d, (d + i) % 4) for d in range(4)])


def from_keys(x):
    return lax.all_to_all(jnp.broadcast_to(x[None], (8,) + x.shape), KEYS, 0, 0, tiled=True)


def to_keys(parts):
    return lax.all_to_all(parts, KEYS, 0, 0, tiled=True)


def after(values, *done):
    return lax.optimization_barrier((values, done))[0]


def swapped(x, axis):
    return lax.ppermute(x, axis, [(0, 1), (1, 0)])


def team_rows(x):
    pair = jnp.concatenate([x, swapped(x, "fsdp")])
    return jnp.concatenate([pair, swapped(pair, "core")])


def _format_first(all_ref, one_ref, two_ref):
    for i in range(16):
        block = all_ref[0, i, 0].astype(F32)
        one_ref[24 * i : 24 * (i + 1), :] = block[:24]
        two_ref[24 * i : 24 * (i + 1), :] = block[24:48]


def format_first(gathered):
    n = gathered.shape[1]
    return pl.pallas_call(
        _format_first,
        grid=(2, 2),
        out_shape=(
            jax.ShapeDtypeStruct((384, FF), F32),
            jax.ShapeDtypeStruct((FF // 2, D), F32),
        ),
        in_specs=[pl.BlockSpec((1, 16, 1, n, D), lambda zh, c: (zh, 0, c, 0, 0))],
        out_specs=(
            pl.BlockSpec((384, D), lambda zh, c: (0, zh * 2 + c)),
            pl.BlockSpec((384, D), lambda zh, c: (c * 2 + zh, 0)),
        ),
        compiler_params=pltpu.CompilerParams(vmem_limit_bytes=VMEM_LIMIT),
        name="format_first",
    )(gathered.reshape(2, 16, 2, n, D))


def _ordered(first, own, other):
    return jnp.where(first, own, other), jnp.where(first, other, own)


def _turn(x, cosine, sine):
    a, b = x[: ROT // 2], x[ROT // 2 : ROT]
    return jnp.concatenate([a * cosine - b * sine, b * cosine + a * sine, x[ROT:]], axis=0)


def _project(
    me, x_ref, dy_ref, wk_ref, wo_ref, wout_ref, own_ref, other_ref, cos_ref, sin_ref,
    n_ref, scale_ref, a_ref, m_ref, vec_ref, *heads,
):
    first = me[0] == 0
    lo, hi = _ordered(first, own_ref[...].astype(F32), other_ref[...].astype(F32))
    vec = jnp.concatenate([lo, hi], axis=1)
    vec_ref[...] = vec
    x = x_ref[...].astype(F32)
    centred = x - jnp.mean(x, axis=1, keepdims=True)
    scale = lax.rsqrt(jnp.mean(centred * centred, axis=1, keepdims=True) + EPS)
    n = centred * scale
    n_ref[...] = n
    scale_ref[...] = jnp.broadcast_to(scale, scale_ref.shape)
    a = n * vec[0:1] + vec[1:2]
    a_ref[...] = a.astype(BF)
    m_ref[...] = (n * vec[2:3] + vec[3:4]).astype(BF)
    keep, rest = _ordered(first, a[:, : D // 2], a[:, D // 2 :])
    qkv = jnp.dot(keep.astype(BF), wk_ref[...], preferred_element_type=F32)
    qkv = qkv + jnp.dot(rest.astype(BF), wo_ref[...], preferred_element_type=F32)
    bias = []
    for p in range(3):
        part = jnp.zeros((1, HW), F32)
        for j in range(4):
            b = p * 4 + j
            src = (lo, hi)[b // 6]
            row = 6 + (b % 6) // 2
            at = (b % 2) * HW
            part = part + jnp.where(me[1] == j, src[row : row + 1, at : at + HW], 0.0)
        bias.append(part)
    qkv = (qkv + jnp.concatenate(bias, axis=1)).T
    d_mixed = lax.dot_general(
        wout_ref[...], dy_ref[...], (((1,), (1,)), ((), ())), preferred_element_type=F32
    ).astype(BF)
    cosine, sine = cos_ref[...], sin_ref[...]
    for h in range(TH):
        kv_ref, qd_ref = heads[h], heads[TH + h]
        rows = [slice(p * HW + h * HEAD, p * HW + (h + 1) * HEAD) for p in range(3)]
        qd_ref[:HEAD] = _turn(qkv[rows[0]], cosine, sine).astype(BF) * jnp.asarray(0.125, BF)
        qd_ref[HEAD:] = d_mixed[h * HEAD : (h + 1) * HEAD]
        kv_ref[:HEAD] = _turn(qkv[rows[1]], cosine, sine).astype(BF)
        kv_ref[HEAD:] = qkv[rows[2]].astype(BF)


def project(me, *args):
    return pl.pallas_call(
        _project,
        out_shape=(
            jax.ShapeDtypeStruct((TEAM_ROWS, D), F32),
            jax.ShapeDtypeStruct((TEAM_ROWS, 128), F32),
            jax.ShapeDtypeStruct((TEAM_ROWS, D), BF),
            jax.ShapeDtypeStruct((TEAM_ROWS, D), BF),
            jax.ShapeDtypeStruct((9, D), F32),
        )
        + (jax.ShapeDtypeStruct((2 * HEAD, TEAM_ROWS), BF),) * (2 * TH),
        in_specs=[pl.BlockSpec(memory_space=pltpu.SMEM)] + _specs(9),
        out_specs=tuple(_specs(5 + 2 * TH)),
        compiler_params=pltpu.CompilerParams(vmem_limit_bytes=VMEM_LIMIT),
        name="project",
    )(me, *args)


SLOT = 128


def _tail(
    me, dq0, dq1, dq2, dkv0, dkv1, dkv2, cos_ref, sin_ref, a_ref, n_ref, dy_ref, mixed_ref,
    w_ref, early_ref, second_ref, dh_ref, small,
):
    cosine, sine = cos_ref[...], -sin_ref[...]
    parts = [_turn(r[...], cosine, sine) for r in (dq0, dq1, dq2)]
    parts += [_turn(r[:HEAD], cosine, sine) for r in (dkv0, dkv1, dkv2)]
    parts += [r[HEAD:] for r in (dkv0, dkv1, dkv2)]
    turned = jnp.concatenate(parts, axis=0).astype(BF)
    grads = jnp.concatenate(
        [
            jnp.dot(turned, a_ref[...], preferred_element_type=F32),
            jnp.dot(mixed_ref[...], dy_ref[...], preferred_element_type=F32),
        ],
        axis=0,
    ).T
    rows = turned.astype(F32).T
    dh = lax.dot_general(
        rows.astype(BF), w_ref[...], (((1,), (1,)), ((), ())), preferred_element_type=F32
    )
    dh_ref[...] = dh
    vectors = [early_ref[i : i + 1] for i in range(4)]
    vectors.append(jnp.sum(dh * n_ref[...], axis=0, keepdims=True))
    vectors.append(jnp.sum(dh, axis=0, keepdims=True))
    bias = jnp.sum(rows, axis=0, keepdims=True)
    for p in range(3):
        part = bias[:, p * HW : (p + 1) * HW]
        vectors.append(
            jnp.concatenate([jnp.where(me[1] == j, part, 0.0) for j in range(4)], axis=1)
        )
    small[...] = jnp.zeros_like(small)
    for v, vector in enumerate(vectors):
        for i in range(6):
            at = v * 6 + i
            small[at % 32, at // 32 : at // 32 + 1, :] = vector[:, i * SLOT : (i + 1) * SLOT]
    for g in range(32):
        second_ref[g, :, :D] = grads[24 * g : 24 * (g + 1)].astype(BF)
        second_ref[g, :, D:] = small[g].astype(BF)


def tail(me, *args):
    return pl.pallas_call(
        _tail,
        out_shape=(
            jax.ShapeDtypeStruct((32, 24, D + SLOT), BF),
            jax.ShapeDtypeStruct((TEAM_ROWS, D), F32),
        ),
        in_specs=[pl.BlockSpec(memory_space=pltpu.SMEM)] + _specs(14),
        out_specs=tuple(_specs(2)),
        scratch_shapes=[pltpu.VMEM((32, 24, SLOT), F32)],
        compiler_params=pltpu.CompilerParams(vmem_limit_bytes=VMEM_LIMIT),
        name="tail",
    )(me, *args)


def _format_second(me, own_ref, other_ref, qkv_ref, out_ref, small_ref):
    first = me[2] == 0
    turned = [[], []]
    for zh in range(2):
        for i in range(16):
            g = zh * 16 + i
            pair = _ordered(first, own_ref[g].astype(F32), other_ref[g].astype(F32))
            for c, block in enumerate(pair):
                h = zh * 2 + c
                for p in range(3):
                    at = p * D + h * HW
                    qkv_ref[24 * i : 24 * (i + 1), at : at + HW] = block[:, p * HW : (p + 1) * HW]
                turned[c].append(block[:, 3 * HW : D])
                for slot in range(2):
                    small_ref[c, slot * 32 + g : slot * 32 + g + 1, :] = block[slot : slot + 1, D:]
    for c in range(2):
        out_ref[c * HW : (c + 1) * HW, :] = jnp.concatenate(turned[c], axis=0).T


def format_second(me, own, other):
    return pl.pallas_call(
        _format_second,
        out_shape=(
            jax.ShapeDtypeStruct((384, 3 * D), F32),
            jax.ShapeDtypeStruct((384, D), F32),
            jax.ShapeDtypeStruct((2, 64, SLOT), F32),
        ),
        in_specs=[pl.BlockSpec(memory_space=pltpu.SMEM)] + _specs(2),
        out_specs=tuple(_specs(3)),
        compiler_params=pltpu.CompilerParams(vmem_limit_bytes=VMEM_LIMIT),
        name="format_second",
    )(me, own, other)


def dot(a, b, dims):
    return lax.dot_general(a, b, (dims, ((), ())), preferred_element_type=F32)


def local(
    tokens,
    block_order,
    cotangent,
    ln_gain_attn,
    ln_bias_attn,
    ln_gain_mlp,
    ln_bias_mlp,
    w_qkv,
    b_qkv,
    w_out,
    b_out,
    w_fc1,
    b_fc1,
    w_fc2,
    b_fc2,
):
    z, xh, y, core, fsdp = (lax.axis_index(a) for a in AXES)
    team = core * 2 + fsdp
    mine = fsdp * 2 + core
    theirs = (1 - fsdp) * 2 + core
    group = (z * 2 + xh) * 4 + y

    def columns(w, which, width):
        return lax.dynamic_slice_in_dim(w, which * width, width, axis=1)

    def qkv_columns(w, which):
        return jnp.concatenate(
            [columns(w[:, i * D : (i + 1) * D], which, HW) for i in range(3)], axis=1
        )

    def ordered(keep, other):
        return (jnp.where(fsdp == 0, keep, other), jnp.where(fsdp == 0, other, keep))

    def whole_rows(keep, send):
        return jnp.concatenate(ordered(keep, swapped(send, "fsdp")))

    me = jnp.stack([fsdp, mine, core]).astype(jnp.int32)

    x4 = team_rows(tokens)
    w_keep = qkv_columns(w_qkv, mine)
    w_rest = swapped(qkv_columns(w_qkv, theirs), "fsdp")
    dy4 = team_rows(cotangent)
    vectors = jnp.concatenate(
        [
            v.reshape(-1, 384)
            for v in (ln_gain_attn, ln_bias_attn, ln_gain_mlp, ln_bias_mlp, b_out, b_fc2, b_qkv)
        ]
    )
    w_o = lax.dynamic_slice_in_dim(w_out, core * HW, HW, axis=0)
    w_one = whole_rows(columns(w_fc1, mine, D), columns(w_fc1, theirs, D))
    w_two = lax.dynamic_slice_in_dim(w_fc2, core * D, D, axis=0)
    b_one = lax.dynamic_slice_in_dim(b_fc1, core * D, D, axis=0).astype(F32)

    fplan, bplan = make_plan(block_order, team, z, xh, y)

    anchors = pick(block_order, group * 4 + (jnp.arange(4, dtype=jnp.int32) ^ team))
    places = (anchors[:, None] * BLK + jnp.arange(BLK, dtype=jnp.int32)[None, :]).reshape(-1)
    frequency = jnp.exp(jnp.arange(ROT // 2, dtype=F32) * (-2.0 * math.log(10000.0) / ROT))
    angles = frequency[:, None] * places.astype(F32)[None, :]
    cosine, sine = jnp.cos(angles), jnp.sin(angles)

    n, scale, a_attn, a_mlp, vec, *heads = project(
        me, x4, dy4, w_keep, w_rest, w_o, vectors, swapped(vectors, "fsdp"), cosine, sine
    )
    kv_all = [from_keys(kv) for kv in heads[:TH]]
    qd_all = [
        jnp.stack([qd] + [from_y(qd, i) for i in range(1, 4)]) for qd in heads[TH:]
    ]
    d_mixed = [qd[HEAD:] for qd in heads[TH:]]

    hidden_pre = dot(a_mlp, w_one, ((1,), (0,))) + b_one
    hidden_act, gelu_pull = jax.vjp(partial(jax.nn.gelu, approximate=False), hidden_pre)
    act = hidden_act.astype(BF)
    out_part = dot(act, w_two, ((1,), (0,)))
    d_act = dot(dy4, w_two, ((1,), (1,)))
    d_hidden = gelu_pull(d_act)[0].astype(BF)
    grad_one = dot(a_mlp, d_hidden, ((0,), (0,)))
    grad_two = dot(act, dy4, ((0,), (0,)))
    grad_b_one = jnp.sum(d_hidden.astype(F32), axis=0)
    dh_mlp = dot(d_hidden, w_one, ((1,), (1,)))

    early = jnp.stack(
        [
            jnp.sum(dh_mlp * n, axis=0),
            jnp.sum(dh_mlp, axis=0),
            jnp.sum(cotangent.astype(F32), axis=0),
            grad_b_one,
        ]
    )
    first = jnp.concatenate(
        [grad_one.astype(BF).reshape(32, 24, D), grad_two.astype(BF).reshape(32, 24, D)], axis=1
    )

    def to_owner(part):
        pairs = []
        for at in range(8):
            zz, f = at // 2, at % 2
            if f == 0 and zz >= 2:
                pairs.append((at, (zz - 2) * 2 + 1))
            elif f == 1 and zz < 2:
                pairs.append((at, (zz + 2) * 2))
            else:
                pairs.append((at, at))
        return lax.ppermute(part, ("z", "fsdp"), pairs)

    def merged(out, h, *done):
        parts = after([out[0]] + [to_y(out[i], i) for i in range(1, 4)], *done)
        parts = jnp.stack(parts).astype(F32)
        lse_parts = jnp.sum(parts[:, HEAD : HEAD + 3], axis=1)
        peak = jnp.max(lse_parts, axis=0)
        share = jnp.exp(lse_parts - peak[None])
        total = jnp.sum(share, axis=0)
        whole = jnp.sum(parts[:, :HEAD] * (share / total[None])[:, None, :], axis=0)
        delta = jnp.sum(whole * d_mixed[h].astype(F32), axis=0)
        return whole, jnp.stack([peak + jnp.log(total), delta] + [jnp.zeros_like(delta)] * 6)

    def stats(ld, *done):
        return jnp.stack(after([ld] + [from_y(ld, i) for i in range(1, 4)], *done))

    def pulled(dq_parts, dkv_parts, *done):
        dkv = to_keys(dkv_parts)
        dq = [dq_parts[0]] + [to_y(dq_parts[i], i) for i in range(1, 4)]
        dkv, dq = after((dkv, dq), *done)
        return sum(part.astype(F32) for part in dq), jnp.sum(dkv.astype(F32), axis=0)

    out_0 = attend_forward(fplan, qd_all[0], kv_all[0])
    out_1 = attend_forward(after(fplan, out_0), qd_all[1], kv_all[1])
    first = lax.all_to_all(after(first, out_1), GROUPS, 0, 0, tiled=True)
    whole_0, ld_0 = merged(out_0, 0, out_1)
    out_2 = attend_forward(after(fplan, out_1, ld_0), qd_all[2], kv_all[2])
    ld_0 = stats(ld_0, out_2)
    whole_1, ld_1 = merged(out_1, 1, out_2)
    raw_0 = attend_backward(after(bplan, out_2, ld_1), qd_all[0], kv_all[0], ld_0)
    ld_1 = stats(ld_1, raw_0)
    whole_2, ld_2 = merged(out_2, 2, raw_0)
    first = jnp.sum(after(first, raw_0).astype(F32), axis=0)
    raw_1 = attend_backward(after(bplan, raw_0, ld_2, first), qd_all[1], kv_all[1], ld_1)
    ld_2 = stats(ld_2, raw_1)
    grads_0 = pulled(*raw_0, raw_1)
    raw_2 = attend_backward(after(bplan, raw_1, grads_0), qd_all[2], kv_all[2], ld_2)
    grads_1 = pulled(*raw_1, raw_2)
    grads_2 = pulled(*raw_2)
    mixed = jnp.concatenate([whole_0, whole_1, whole_2]).astype(BF)

    first = jnp.concatenate([to_owner(first[:24].astype(BF)), first[24:].astype(BF)], axis=0)
    first_all = lax.all_gather(first, CTX, axis=0, tiled=False)

    w_q = jnp.concatenate(ordered(w_keep, w_rest))
    second, dh_attn = tail(
        me,
        *(dq for dq, _ in (grads_0, grads_1, grads_2)),
        *(dkv for _, dkv in (grads_0, grads_1, grads_2)),
        cosine,
        sine,
        a_attn,
        n,
        dy4,
        mixed,
        w_q,
        early,
    )
    second = jnp.sum(lax.all_to_all(second, GROUPS, 0, 0, tiled=True).astype(F32), axis=0)
    shares = second[:, D:]
    whole = (jnp.arange(24, dtype=jnp.int32)[:, None] == 0) & (group >= 18) & (group < 24)
    shares = shares + jnp.where(whole, 0.0, swapped(shares, "fsdp"))
    second = second.astype(BF)
    second = jnp.concatenate(
        [to_owner(second[:, : 3 * HW]), second[:, 3 * HW : D], shares.astype(BF)], axis=1
    )
    sent = jnp.broadcast_to(second[None], (32,) + second.shape)
    second = lax.all_to_all(sent, GROUPS, 0, 0, tiled=True)
    second_other = swapped(second, "core")

    out_part = out_part + dot(mixed, w_o, ((0,), (0,)))
    dn_part = dh_attn * vec[0:1] + dh_mlp * vec[2:3]
    both = jnp.concatenate([out_part, dn_part], axis=1).reshape(4, BLK, 2 * D)
    both = both[:2] + swapped(both[2:].astype(BF), "core").astype(F32)
    both = both[0] + swapped(both[1].astype(BF), "fsdp").astype(F32)
    layer_out = (tokens.astype(F32) + both[:, :D] + vec[4:5] + vec[5:6]).astype(BF)
    dn = both[:, D:]
    grad_tokens = cotangent.astype(F32) + scale[:BLK, :1] * (
        dn
        - jnp.mean(dn, axis=1, keepdims=True)
        - n[:BLK] * jnp.mean(dn * n[:BLK], axis=1, keepdims=True)
    )

    grad_w_one, grad_w_two = format_first(first_all)
    grad_w_qkv, grad_w_out, small = format_second(me, second, second_other)
    summed = small[0] + small[1]

    def half(at, rows):
        return lax.dynamic_slice_in_dim(summed[at : at + rows], fsdp * (rows // 2), rows // 2).reshape(-1)

    grad_b_out = half(12, 6)
    return (
        layer_out,
        grad_tokens,
        half(24, 6),
        half(30, 6),
        half(0, 6),
        half(6, 6),
        grad_w_qkv,
        half(36, 18),
        grad_w_out,
        grad_b_out,
        grad_w_one,
        small[:, 18:24].reshape(-1),
        grad_w_two,
        grad_b_out,
    )


def solution(mesh):
    fine = Mesh(mesh.devices.reshape(SIZES), AXES)
    rows = P(AXES, None)
    vec = P("fsdp")
    mat = P("fsdp", None)
    return jax.shard_map(
        local,
        mesh=fine,
        in_specs=(
            rows, P(), rows, vec, vec, vec, vec, mat, vec, mat, vec, mat, vec, mat, vec,
        ),
        out_specs=(
            rows, rows, vec, vec, vec, vec, mat, vec, mat, vec, mat, vec, mat, vec,
        ),
        check_vma=False,
    )
```

```python
from functools import partial
import math

import jax
import jax.numpy as jnp
from jax import lax
from jax.experimental import pallas as pl
from jax.experimental.pallas import tpu as pltpu
from jax.sharding import Mesh, PartitionSpec as P

HEADS = 12
HEAD = 64
ROT = 16
D = 768
FF = 3072
BLK = 128
EPS = 1e-05
MASKED = -1e30
FLOOR = -1e20

AXES = ("z", "xh", "y", "core", "fsdp")
SIZES = (4, 2, 4, 2, 2)
CTX = ("z", "xh", "y", "core")
TEAM = ("core", "fsdp")
KEYS = ("z", "xh")
GROUPS = ("z", "xh", "y")

NH = 1
TH = 3
HW = TH * HEAD
KW = NH * HEAD
TEAM_ROWS = 512
NQ = 16
NK = 32
QT = 2
FQT = 4
CH = 4
PAIR = 2
FPAIR = 2
UNROLL = 8
BF = jnp.bfloat16
F32 = jnp.float32
VMEM_LIMIT = 56 * 1024 * 1024


def _sort_keys(kv_ref, ksrc, kvt, kn):
    def step(r, _):
        src = ksrc[r]
        at = pl.multiple_of((src % 4) * BLK, BLK)
        to = pl.multiple_of(r * BLK, BLK)
        blk = kv_ref[src // 4, :, pl.ds(at, BLK)]
        kvt[:, pl.ds(to, BLK)] = blk
        for h in range(NH):
            kn[h, pl.ds(to, BLK), :] = blk[2 * HEAD * h : 2 * HEAD * (h + 1)].T
        return 0

    lax.fori_loop(0, NK, step, 0, unroll=UNROLL)


def _head_rows(head):
    return slice(2 * HEAD * head, 2 * HEAD * (head + 1))


def _tile_columns(ref, qsrc, t, rows, qt):
    parts = []
    for i in range(qt):
        src = qsrc[t * qt + i]
        at = pl.multiple_of((src % 4) * BLK, BLK)
        parts.append(ref[src // 4, rows, pl.ds(at, BLK)])
    return jnp.concatenate(parts, axis=1)


def _allowed(kpos, qpos, t, c, qt):
    row = lax.broadcasted_iota(jnp.int32, (BLK, qt * BLK), 0)
    col = lax.broadcasted_iota(jnp.int32, (BLK, BLK), 1)
    query = jnp.concatenate([qpos[t * qt + i] * BLK + col for i in range(qt)], axis=1)
    return jnp.concatenate([kpos[c * CH + i] * BLK + row <= query for i in range(CH)], axis=0)


def _forward(head, qsrc, qpos, ksrc, kpos, nfull, nall, qd_ref, kv_ref, o_ref, kvt, kn):
    _sort_keys(kv_ref, ksrc, kvt, kn)
    width = FQT * BLK

    def tile(t, _):
        blk = _tile_columns(qd_ref, qsrc, t, _head_rows(head), FQT)
        half = lax.broadcasted_iota(jnp.int32, (2 * HEAD, width), 0) < HEAD
        zero = jnp.zeros((2 * HEAD, width), BF)
        queries = [
            jnp.where(half, blk[2 * HEAD * h : 2 * HEAD * (h + 1)], zero) for h in range(NH)
        ]

        def chunk(masked, step, c, carry):
            rows = step * CH * BLK
            at = pl.multiple_of(c * rows, rows)
            out = []
            if masked:
                ok = _allowed(kpos, qpos, t, c, FQT)
            for h in range(NH):
                m, l, acc = carry[h]
                s = jnp.dot(kn[h, pl.ds(at, rows), :], queries[h], preferred_element_type=F32)
                if masked:
                    s = jnp.where(ok, s, MASKED)
                new = jnp.maximum(m, jnp.max(s, axis=0, keepdims=True))
                p = jnp.exp(s - new)
                fade = jnp.exp(m - new)
                l = l * fade + jnp.sum(p, axis=0, keepdims=True)
                v = kvt[2 * HEAD * h + HEAD : 2 * HEAD * (h + 1), pl.ds(at, rows)]
                acc = acc * fade + jnp.dot(v, p.astype(BF), preferred_element_type=F32)
                out.append((new, l, acc))
            return tuple(out)

        start = tuple(
            (
                jnp.full((1, width), FLOOR, F32),
                jnp.zeros((1, width), F32),
                jnp.zeros((HEAD, width), F32),
            )
            for _ in range(NH)
        )
        wide = nfull[t] // FPAIR
        state = lax.fori_loop(0, wide, partial(chunk, False, FPAIR), start)
        state = lax.fori_loop(wide * FPAIR, nfull[t], partial(chunk, False, 1), state)
        state = lax.fori_loop(nfull[t], nall[t], partial(chunk, True, 1), state)
        stats = []
        for h in range(NH):
            m, l, acc = state[h]
            some = l > 0.0
            safe = jnp.where(some, l, 1.0)
            o = (acc / safe).astype(BF)
            lse = jnp.where(some, m + jnp.log(safe), FLOOR)
            hi = lse.astype(BF)
            rest = lse - hi.astype(F32)
            mid = rest.astype(BF)
            low = (rest - mid.astype(F32)).astype(BF)
            stats += [hi.astype(F32), mid.astype(F32), low.astype(F32)]
            for i in range(FQT):
                src = qsrc[t * FQT + i]
                at = pl.multiple_of((src % 4) * BLK, BLK)
                o_ref[src // 4, HEAD * h : HEAD * (h + 1), pl.ds(at, BLK)] = o[:, i * BLK : (i + 1) * BLK]
        stats = jnp.concatenate(stats + [jnp.zeros((16 - 3 * NH, width), F32)], axis=0).astype(BF)
        for i in range(FQT):
            src = qsrc[t * FQT + i]
            at = pl.multiple_of((src % 4) * BLK, BLK)
            o_ref[src // 4, KW : KW + 16, pl.ds(at, BLK)] = stats[:, i * BLK : (i + 1) * BLK]
        return 0

    lax.fori_loop(0, NQ // FQT, tile, 0)


def _row_stats(parts, src, grad):
    at = pl.multiple_of((src % 4) * BLK, BLK)
    outs, sums = [], []
    for i, ref in enumerate(parts):
        part = ref[(src // 4 + 4 - i) % 4, :, pl.ds(at, BLK)].astype(F32)
        outs.append(part[:HEAD])
        sums.append(part[HEAD : HEAD + 1] + part[HEAD + 1 : HEAD + 2] + part[HEAD + 2 : HEAD + 3])
    peak = jnp.maximum(jnp.maximum(sums[0], sums[1]), jnp.maximum(sums[2], sums[3]))
    shares = [jnp.exp(x - peak) for x in sums]
    total = shares[0] + shares[1] + shares[2] + shares[3]
    whole = sum(o * (x / total) for o, x in zip(outs, shares))
    return peak + jnp.log(total), jnp.sum(whole * grad, axis=0, keepdims=True)


def _backward(
    head, qsrc, qpos, ksrc, kpos, nfull, nall, qd_ref, kv_ref, o0, o1, o2, o3, dq_ref, dkv_ref,
    kvt, kn, acc, w1, w2, dq,
):
    _sort_keys(kv_ref, ksrc, kvt, kn)
    width = QT * BLK
    acc[...] = jnp.zeros_like(acc)

    def tile(t, _):
        blk = _tile_columns(qd_ref, qsrc, t, _head_rows(head), QT)
        stats = []
        for i in range(QT):
            grad = blk[HEAD:, i * BLK : (i + 1) * BLK].astype(F32)
            stats.append(_row_stats((o0, o1, o2, o3), qsrc[t * QT + i], grad))
        stats = [jnp.concatenate(part, axis=1) for part in zip(*stats)]
        top = lax.broadcasted_iota(jnp.int32, (2 * HEAD, width), 0) < HEAD
        left = lax.broadcasted_iota(jnp.int32, (width, 2 * HEAD), 1) < HEAD
        zero = jnp.zeros((2 * HEAD, width), BF)
        zero_t = jnp.zeros((width, 2 * HEAD), BF)
        for h in range(NH):
            both = blk[2 * HEAD * h : 2 * HEAD * (h + 1)]
            w1[h, :, :width] = jnp.where(top, both, zero)
            w1[h, :, width:] = jnp.where(top, zero, both)
            turned = both.T
            w2[h, :width, :] = jnp.where(left, turned, zero_t)
            w2[h, width:, :] = jnp.where(left, zero_t, turned)
        dq[...] = jnp.zeros_like(dq)

        def chunk(masked, step, c, _):
            rows = step * CH * BLK
            at = pl.multiple_of(c * rows, rows)
            if masked:
                ok = _allowed(kpos, qpos, t, c, QT)
            for h in range(NH):
                sd = jnp.dot(kn[h, pl.ds(at, rows), :], w1[h], preferred_element_type=F32)
                s = sd[:, :width]
                if masked:
                    s = jnp.where(ok, s, MASKED)
                p = jnp.exp(s - stats[0])
                ds = (p * (sd[:, width:] - stats[1])).astype(BF)
                pd = jnp.concatenate([ds, p.astype(BF)], axis=1)
                acc[h, pl.ds(at, rows), :] += jnp.dot(pd, w2[h], preferred_element_type=F32)
                k = kvt[2 * HEAD * h : 2 * HEAD * h + HEAD, pl.ds(at, rows)]
                dq[h] += jnp.dot(k, ds, preferred_element_type=F32)
            return 0

        wide = nfull[t] // PAIR
        lax.fori_loop(0, wide, partial(chunk, False, PAIR), 0)
        lax.fori_loop(wide * PAIR, nfull[t], partial(chunk, False, 1), 0)
        lax.fori_loop(nfull[t], nall[t], partial(chunk, True, 1), 0)
        for h in range(NH):
            out = (dq[h] * 0.125).astype(BF)
            for i in range(QT):
                src = qsrc[t * QT + i]
                at = pl.multiple_of((src % 4) * BLK, BLK)
                dq_ref[src // 4, HEAD * h : HEAD * (h + 1), pl.ds(at, BLK)] = out[:, i * BLK : (i + 1) * BLK]
        return 0

    lax.fori_loop(0, NQ // QT, tile, 0)

    def back(r, _):
        src = ksrc[r]
        at = pl.multiple_of((src % 4) * BLK, BLK)
        for h in range(NH):
            part = acc[h, pl.ds(pl.multiple_of(r * BLK, BLK), BLK), :].T.astype(BF)
            dkv_ref[src // 4, 2 * HEAD * h : 2 * HEAD * (h + 1), pl.ds(at, BLK)] = part
        return 0

    lax.fori_loop(0, NK, back, 0, unroll=UNROLL)


def _specs(n):
    return [pl.BlockSpec(memory_space=pltpu.VMEM)] * n


def attend_forward(head, plan, qd, kv):
    return pl.pallas_call(
        partial(_forward, head),
        out_shape=jax.ShapeDtypeStruct((4, KW + 16, TEAM_ROWS), BF),
        in_specs=[pl.BlockSpec(memory_space=pltpu.SMEM)] * 6 + _specs(2),
        out_specs=pl.BlockSpec(memory_space=pltpu.VMEM),
        scratch_shapes=[
            pltpu.VMEM((2 * KW, NK * BLK), BF),
            pltpu.VMEM((NH, NK * BLK, 2 * HEAD), BF),
        ],
        compiler_params=pltpu.CompilerParams(vmem_limit_bytes=VMEM_LIMIT),
        cost_estimate=pl.CostEstimate(flops=4 * NH * NQ * NK * BLK * BLK * HEAD, bytes_accessed=4 * NH * (NQ + NK) * BLK * BLK, transcendentals=NH * NQ * NK * BLK * BLK),
        name="attend_forward",
    )(*plan, qd, kv)


def attend_backward(head, plan, qd, kv, parts):
    width = QT * BLK
    return pl.pallas_call(
        partial(_backward, head),
        out_shape=(
            jax.ShapeDtypeStruct((4, KW, TEAM_ROWS), BF),
            jax.ShapeDtypeStruct((8, 2 * KW, TEAM_ROWS), BF),
        ),
        in_specs=[pl.BlockSpec(memory_space=pltpu.SMEM)] * 6 + _specs(6),
        out_specs=tuple(_specs(2)),
        scratch_shapes=[
            pltpu.VMEM((2 * KW, NK * BLK), BF),
            pltpu.VMEM((NH, NK * BLK, 2 * HEAD), BF),
            pltpu.VMEM((NH, NK * BLK, 2 * HEAD), F32),
            pltpu.VMEM((NH, 2 * HEAD, 2 * width), BF),
            pltpu.VMEM((NH, 2 * width, 2 * HEAD), BF),
            pltpu.VMEM((NH, HEAD, width), F32),
        ],
        compiler_params=pltpu.CompilerParams(vmem_limit_bytes=VMEM_LIMIT),
        cost_estimate=pl.CostEstimate(flops=10 * NH * NQ * NK * BLK * BLK * HEAD, bytes_accessed=8 * NH * (NQ + NK) * BLK * BLK, transcendentals=NH * NQ * NK * BLK * BLK),
        name="attend_backward",
    )(*plan, qd, kv, *parts)


def pick(table, index):
    ids = jnp.arange(table.shape[0], dtype=jnp.int32)
    return jnp.sum(jnp.where(index[:, None] == ids[None, :], table[None, :], 0), axis=1)


def in_order(pos):
    ids = jnp.arange(pos.shape[0], dtype=jnp.int32)
    rank = jnp.sum((pos[None, :] < pos[:, None]).astype(jnp.int32), axis=1)
    hit = rank[None, :] == ids[:, None]
    return (
        jnp.sum(jnp.where(hit, ids[None, :], 0), axis=1),
        jnp.sum(jnp.where(hit, pos[None, :], 0), axis=1),
    )


def make_plan(block_order, team, z, xh, y):
    rows = jnp.arange(4, dtype=jnp.int32) ^ team
    other = (y + jnp.arange(4, dtype=jnp.int32)) % 4
    mine = ((z * 2 + xh) * 4 + other)[:, None] * 4 + rows[None, :]
    theirs = (jnp.arange(8, dtype=jnp.int32) * 4 + y)[:, None] * 4 + rows[None, :]
    qsrc, qpos = in_order(pick(block_order, mine.reshape(-1)))
    ksrc, kpos = in_order(pick(block_order, theirs.reshape(-1)))

    def plan(qt):
        ends = qpos.reshape(NQ // qt, qt)
        below = jnp.sum((kpos[None, :] < ends[:, :1]).astype(jnp.int32), axis=1)
        upto = jnp.sum((kpos[None, :] <= ends[:, -1:]).astype(jnp.int32), axis=1)
        return (qsrc, qpos, ksrc, kpos, below // CH, (upto + CH - 1) // CH)

    return plan(FQT), plan(QT)


def from_y(x, i):
    return lax.ppermute(x, "y", [((d + i) % 4, d) for d in range(4)])


def to_y(x, i):
    return lax.ppermute(x, "y", [(d, (d + i) % 4) for d in range(4)])


def from_keys(x):
    return lax.all_to_all(jnp.broadcast_to(x[None], (8,) + x.shape), KEYS, 0, 0, tiled=True)


def to_keys(parts):
    return lax.all_to_all(parts, KEYS, 0, 0, tiled=True)


def after(values, *done):
    return lax.optimization_barrier((values, done))[0]


def swapped(x, axis):
    return lax.ppermute(x, axis, [(0, 1), (1, 0)])


def team_rows(x):
    pair = jnp.concatenate([x, swapped(x, "fsdp")])
    return jnp.concatenate([pair, swapped(pair, "core")])


def _format_first(all_ref, one_ref, two_ref):
    for i in range(16):
        block = all_ref[0, i, 0].astype(F32)
        one_ref[24 * i : 24 * (i + 1), :] = block[:24]
        two_ref[24 * i : 24 * (i + 1), :] = block[24:48]


def format_first(gathered):
    n = gathered.shape[1]
    return pl.pallas_call(
        _format_first,
        grid=(2, 2),
        out_shape=(
            jax.ShapeDtypeStruct((384, FF), F32),
            jax.ShapeDtypeStruct((FF // 2, D), F32),
        ),
        in_specs=[pl.BlockSpec((1, 16, 1, n, D), lambda zh, c: (zh, 0, c, 0, 0))],
        out_specs=(
            pl.BlockSpec((384, D), lambda zh, c: (0, zh * 2 + c)),
            pl.BlockSpec((384, D), lambda zh, c: (c * 2 + zh, 0)),
        ),
        compiler_params=pltpu.CompilerParams(vmem_limit_bytes=VMEM_LIMIT),
        name="format_first",
    )(gathered.reshape(2, 16, 2, n, D))


def _ordered(first, own, other):
    return jnp.where(first, own, other), jnp.where(first, other, own)


def _turn(x, cosine, sine):
    a, b = x[: ROT // 2], x[ROT // 2 : ROT]
    return jnp.concatenate([a * cosine - b * sine, b * cosine + a * sine, x[ROT:]], axis=0)


def _project(
    me, x_ref, dy_ref, wk_ref, wo_ref, wout_ref, own_ref, other_ref, cos_ref, sin_ref,
    n_ref, scale_ref, a_ref, m_ref, vec_ref, *heads,
):
    first = me[0] == 0
    lo, hi = _ordered(first, own_ref[...].astype(F32), other_ref[...].astype(F32))
    vec = jnp.concatenate([lo, hi], axis=1)
    vec_ref[...] = vec
    x = x_ref[...].astype(F32)
    centred = x - jnp.mean(x, axis=1, keepdims=True)
    scale = lax.rsqrt(jnp.mean(centred * centred, axis=1, keepdims=True) + EPS)
    n = centred * scale
    n_ref[...] = n
    scale_ref[...] = jnp.broadcast_to(scale, scale_ref.shape)
    a = n * vec[0:1] + vec[1:2]
    a_ref[...] = a.astype(BF)
    m_ref[...] = (n * vec[2:3] + vec[3:4]).astype(BF)
    keep, rest = _ordered(first, a[:, : D // 2], a[:, D // 2 :])
    qkv = jnp.dot(keep.astype(BF), wk_ref[...], preferred_element_type=F32)
    qkv = qkv + jnp.dot(rest.astype(BF), wo_ref[...], preferred_element_type=F32)
    bias = []
    for p in range(3):
        part = jnp.zeros((1, HW), F32)
        for j in range(4):
            b = p * 4 + j
            src = (lo, hi)[b // 6]
            row = 6 + (b % 6) // 2
            at = (b % 2) * HW
            part = part + jnp.where(me[1] == j, src[row : row + 1, at : at + HW], 0.0)
        bias.append(part)
    qkv = (qkv + jnp.concatenate(bias, axis=1)).T
    d_mixed = lax.dot_general(
        wout_ref[...], dy_ref[...], (((1,), (1,)), ((), ())), preferred_element_type=F32
    ).astype(BF)
    cosine, sine = cos_ref[...], sin_ref[...]
    for h in range(TH):
        kv_ref, qd_ref = heads[h], heads[TH].at[_head_rows(h)]
        rows = [slice(p * HW + h * HEAD, p * HW + (h + 1) * HEAD) for p in range(3)]
        qd_ref[:HEAD] = _turn(qkv[rows[0]], cosine, sine).astype(BF) * jnp.asarray(0.125, BF)
        qd_ref[HEAD:] = d_mixed[h * HEAD : (h + 1) * HEAD]
        kv_ref[:HEAD] = _turn(qkv[rows[1]], cosine, sine).astype(BF)
        kv_ref[HEAD:] = qkv[rows[2]].astype(BF)


def project(me, *args):
    return pl.pallas_call(
        _project,
        out_shape=(
            jax.ShapeDtypeStruct((TEAM_ROWS, D), F32),
            jax.ShapeDtypeStruct((TEAM_ROWS, 128), F32),
            jax.ShapeDtypeStruct((TEAM_ROWS, D), BF),
            jax.ShapeDtypeStruct((TEAM_ROWS, D), BF),
            jax.ShapeDtypeStruct((9, D), F32),
        )
        + (jax.ShapeDtypeStruct((2 * HEAD, TEAM_ROWS), BF),) * TH
        + (jax.ShapeDtypeStruct((2 * HW, TEAM_ROWS), BF),),
        in_specs=[pl.BlockSpec(memory_space=pltpu.SMEM)] + _specs(9),
        out_specs=tuple(_specs(6 + TH)),
        compiler_params=pltpu.CompilerParams(vmem_limit_bytes=VMEM_LIMIT),
        name="project",
    )(me, *args)


SLOT = 128


def _tail(
    me, dq_ref, dkv0_ref, dkv_ref, cos_ref, sin_ref, a_ref, n_ref, dy_ref, mixed_ref,
    w_ref, early_ref, second_ref, dh_ref, small,
):
    cosine, sine = cos_ref[...], -sin_ref[...]
    keys = [dkv0_ref[...], dkv_ref[: 2 * HEAD], dkv_ref[2 * HEAD :]]
    parts = [_turn(dq_ref[h * HEAD : (h + 1) * HEAD], cosine, sine) for h in range(TH)]
    parts += [_turn(x[:HEAD], cosine, sine) for x in keys]
    parts += [x[HEAD:] for x in keys]
    turned = jnp.concatenate(parts, axis=0).astype(BF)
    grads = jnp.concatenate(
        [
            jnp.dot(turned, a_ref[...], preferred_element_type=F32),
            jnp.dot(mixed_ref[...], dy_ref[...], preferred_element_type=F32),
        ],
        axis=0,
    ).T
    rows = turned.astype(F32).T
    dh = lax.dot_general(
        rows.astype(BF), w_ref[...], (((1,), (1,)), ((), ())), preferred_element_type=F32
    )
    dh_ref[...] = dh
    vectors = [early_ref[i : i + 1] for i in range(4)]
    vectors.append(jnp.sum(dh * n_ref[...], axis=0, keepdims=True))
    vectors.append(jnp.sum(dh, axis=0, keepdims=True))
    bias = jnp.sum(rows, axis=0, keepdims=True)
    for p in range(3):
        part = bias[:, p * HW : (p + 1) * HW]
        vectors.append(
            jnp.concatenate([jnp.where(me[1] == j, part, 0.0) for j in range(4)], axis=1)
        )
    small[...] = jnp.zeros_like(small)
    for v, vector in enumerate(vectors):
        for i in range(6):
            at = v * 6 + i
            small[at % 32, at // 32 : at // 32 + 1, :] = vector[:, i * SLOT : (i + 1) * SLOT]
    for g in range(32):
        second_ref[g, :, :D] = grads[24 * g : 24 * (g + 1)].astype(BF)
        second_ref[g, :, D:] = small[g].astype(BF)


def tail(me, *args):
    return pl.pallas_call(
        _tail,
        out_shape=(
            jax.ShapeDtypeStruct((32, 24, D + SLOT), BF),
            jax.ShapeDtypeStruct((TEAM_ROWS, D), F32),
        ),
        in_specs=[pl.BlockSpec(memory_space=pltpu.SMEM)] + _specs(11),
        out_specs=tuple(_specs(2)),
        scratch_shapes=[pltpu.VMEM((32, 24, SLOT), F32)],
        compiler_params=pltpu.CompilerParams(vmem_limit_bytes=VMEM_LIMIT),
        name="tail",
    )(me, *args)


def _format_second(me, own_ref, other_ref, qkv_ref, out_ref, small_ref):
    first = me[2] == 0
    turned = [[], []]
    for zh in range(2):
        for i in range(16):
            g = zh * 16 + i
            pair = _ordered(first, own_ref[g].astype(F32), other_ref[g].astype(F32))
            for c, block in enumerate(pair):
                h = zh * 2 + c
                for p in range(3):
                    at = p * D + h * HW
                    qkv_ref[24 * i : 24 * (i + 1), at : at + HW] = block[:, p * HW : (p + 1) * HW]
                turned[c].append(block[:, 3 * HW : D])
                for slot in range(2):
                    small_ref[c, slot * 32 + g : slot * 32 + g + 1, :] = block[slot : slot + 1, D:]
    for c in range(2):
        out_ref[c * HW : (c + 1) * HW, :] = jnp.concatenate(turned[c], axis=0).T


def format_second(me, own, other):
    return pl.pallas_call(
        _format_second,
        out_shape=(
            jax.ShapeDtypeStruct((384, 3 * D), F32),
            jax.ShapeDtypeStruct((384, D), F32),
            jax.ShapeDtypeStruct((2, 64, SLOT), F32),
        ),
        in_specs=[pl.BlockSpec(memory_space=pltpu.SMEM)] + _specs(2),
        out_specs=tuple(_specs(3)),
        compiler_params=pltpu.CompilerParams(vmem_limit_bytes=VMEM_LIMIT),
        name="format_second",
    )(me, own, other)


def dot(a, b, dims):
    return lax.dot_general(a, b, (dims, ((), ())), preferred_element_type=F32)


def local(
    tokens,
    block_order,
    cotangent,
    ln_gain_attn,
    ln_bias_attn,
    ln_gain_mlp,
    ln_bias_mlp,
    w_qkv,
    b_qkv,
    w_out,
    b_out,
    w_fc1,
    b_fc1,
    w_fc2,
    b_fc2,
):
    z, xh, y, core, fsdp = (lax.axis_index(a) for a in AXES)
    team = core * 2 + fsdp
    mine = fsdp * 2 + core
    theirs = (1 - fsdp) * 2 + core
    group = (z * 2 + xh) * 4 + y

    def columns(w, which, width):
        return lax.dynamic_slice_in_dim(w, which * width, width, axis=1)

    def qkv_columns(w, which):
        return jnp.concatenate(
            [columns(w[:, i * D : (i + 1) * D], which, HW) for i in range(3)], axis=1
        )

    def ordered(keep, other):
        return (jnp.where(fsdp == 0, keep, other), jnp.where(fsdp == 0, other, keep))

    def whole_rows(keep, send):
        return jnp.concatenate(ordered(keep, swapped(send, "fsdp")))

    me = jnp.stack([fsdp, mine, core]).astype(jnp.int32)

    x4 = team_rows(tokens)
    w_keep = qkv_columns(w_qkv, mine)
    w_rest = swapped(qkv_columns(w_qkv, theirs), "fsdp")
    dy4 = team_rows(cotangent)
    vectors = jnp.concatenate(
        [
            v.reshape(-1, 384)
            for v in (ln_gain_attn, ln_bias_attn, ln_gain_mlp, ln_bias_mlp, b_out, b_fc2, b_qkv)
        ]
    )
    w_o = lax.dynamic_slice_in_dim(w_out, core * HW, HW, axis=0)
    w_one = whole_rows(columns(w_fc1, mine, D), columns(w_fc1, theirs, D))
    w_two = lax.dynamic_slice_in_dim(w_fc2, core * D, D, axis=0)
    b_one = lax.dynamic_slice_in_dim(b_fc1, core * D, D, axis=0).astype(F32)

    fplan, bplan = make_plan(block_order, team, z, xh, y)

    anchors = pick(block_order, group * 4 + (jnp.arange(4, dtype=jnp.int32) ^ team))
    places = (anchors[:, None] * BLK + jnp.arange(BLK, dtype=jnp.int32)[None, :]).reshape(-1)
    frequency = jnp.exp(jnp.arange(ROT // 2, dtype=F32) * (-2.0 * math.log(10000.0) / ROT))
    angles = frequency[:, None] * places.astype(F32)[None, :]
    cosine, sine = jnp.cos(angles), jnp.sin(angles)

    n, scale, a_attn, a_mlp, vec, *heads = project(
        me, x4, dy4, w_keep, w_rest, w_o, vectors, swapped(vectors, "fsdp"), cosine, sine
    )
    *kvs, qd = heads
    kv_0, kv_1 = from_keys(kvs[0]), from_keys(kvs[1])
    qd_all = jnp.stack([qd] + [from_y(qd, i) for i in range(1, 4)])

    hidden_pre = dot(a_mlp, w_one, ((1,), (0,))) + b_one
    hidden_act, gelu_pull = jax.vjp(partial(jax.nn.gelu, approximate=False), hidden_pre)
    act = hidden_act.astype(BF)
    out_part = dot(act, w_two, ((1,), (0,)))
    d_act = dot(dy4, w_two, ((1,), (1,)))
    d_hidden = gelu_pull(d_act)[0].astype(BF)
    grad_one = dot(a_mlp, d_hidden, ((0,), (0,)))
    grad_two = dot(act, dy4, ((0,), (0,)))
    grad_b_one = jnp.sum(d_hidden.astype(F32), axis=0)
    dh_mlp = dot(d_hidden, w_one, ((1,), (1,)))

    early = jnp.stack(
        [
            jnp.sum(dh_mlp * n, axis=0),
            jnp.sum(dh_mlp, axis=0),
            jnp.sum(cotangent.astype(F32), axis=0),
            grad_b_one,
        ]
    )
    first = jnp.concatenate(
        [grad_one.astype(BF).reshape(32, 24, D), grad_two.astype(BF).reshape(32, 24, D)], axis=1
    )

    def to_owner(part):
        pairs = []
        for at in range(8):
            zz, f = at // 2, at % 2
            if f == 0 and zz >= 2:
                pairs.append((at, (zz - 2) * 2 + 1))
            elif f == 1 and zz < 2:
                pairs.append((at, (zz + 2) * 2))
            else:
                pairs.append((at, at))
        return lax.ppermute(part, ("z", "fsdp"), pairs)

    def spread(out, *done):
        return after([out] + [from_y(out, i) for i in range(1, 4)], *done)

    def merged(parts):
        own = jnp.stack([part[-i % 4] for i, part in enumerate(parts)]).astype(F32)
        lse = jnp.sum(own[:, HEAD : HEAD + 3], axis=1)
        share = jnp.exp(lse - jnp.max(lse, axis=0))
        share = share / jnp.sum(share, axis=0)
        return jnp.sum(own[:, :HEAD] * share[:, None, :], axis=0).astype(BF)

    out_0 = attend_forward(0, fplan, qd_all, kv_0)
    kv_1, kv_2 = after((kv_1, kvs[2]), out_0)
    kv_2 = from_keys(kv_2)
    out_1 = attend_forward(1, after(fplan, out_0), qd_all, kv_1)
    first = lax.all_to_all(after(first, out_1), GROUPS, 0, 0, tiled=True)
    kv_2 = after(kv_2, out_1)
    out_2 = attend_forward(2, after(fplan, out_1), qd_all, kv_2)
    parts_0 = spread(out_0, out_2)
    raw_0 = attend_backward(0, after(bplan, out_2), qd_all, kv_0, parts_0)
    parts_1 = spread(out_1, raw_0)
    first = jnp.sum(after(first, raw_0).astype(F32), axis=0)
    raw_1 = attend_backward(1, after(bplan, raw_0, first), qd_all, kv_1, parts_1)
    parts_2 = spread(out_2, raw_1)
    dkv_0 = jnp.sum(after(to_keys(raw_0[1]), raw_1).astype(F32), axis=0)
    raw_2 = attend_backward(2, after(bplan, raw_1, dkv_0), qd_all, kv_2, parts_2)
    dkv = to_keys(jnp.concatenate([raw_1[1], raw_2[1]], axis=1))
    dkv = jnp.sum(dkv.astype(F32), axis=0)
    dq = jnp.concatenate([raw_0[0], raw_1[0], raw_2[0]], axis=1)
    dq = [dq[0]] + [to_y(dq[i], i) for i in range(1, 4)]
    dq = sum(part.astype(F32) for part in dq)
    mixed = jnp.concatenate([merged(parts) for parts in (parts_0, parts_1, parts_2)])

    first = jnp.concatenate([to_owner(first[:24].astype(BF)), first[24:].astype(BF)], axis=0)
    first_all = lax.all_gather(first, CTX, axis=0, tiled=False)

    w_q = jnp.concatenate(ordered(w_keep, w_rest))
    second, dh_attn = tail(
        me,
        dq,
        dkv_0,
        dkv,
        cosine,
        sine,
        a_attn,
        n,
        dy4,
        mixed,
        w_q,
        early,
    )
    second = jnp.sum(lax.all_to_all(second, GROUPS, 0, 0, tiled=True).astype(F32), axis=0)
    shares = second[:, D:]
    whole = (jnp.arange(24, dtype=jnp.int32)[:, None] == 0) & (group >= 18) & (group < 24)
    shares = shares + jnp.where(whole, 0.0, swapped(shares, "fsdp"))
    second = second.astype(BF)
    second = jnp.concatenate(
        [to_owner(second[:, : 3 * HW]), second[:, 3 * HW : D], shares.astype(BF)], axis=1
    )
    sent = jnp.broadcast_to(second[None], (32,) + second.shape)
    second = lax.all_to_all(sent, GROUPS, 0, 0, tiled=True)
    second_other = swapped(second, "core")

    out_part = out_part + dot(mixed, w_o, ((0,), (0,)))
    dn_part = dh_attn * vec[0:1] + dh_mlp * vec[2:3]
    both = jnp.concatenate([out_part, dn_part], axis=1).reshape(4, BLK, 2 * D)
    both = both[:2] + swapped(both[2:].astype(BF), "core").astype(F32)
    both = both[0] + swapped(both[1].astype(BF), "fsdp").astype(F32)
    layer_out = (tokens.astype(F32) + both[:, :D] + vec[4:5] + vec[5:6]).astype(BF)
    dn = both[:, D:]
    grad_tokens = cotangent.astype(F32) + scale[:BLK, :1] * (
        dn
        - jnp.mean(dn, axis=1, keepdims=True)
        - n[:BLK] * jnp.mean(dn * n[:BLK], axis=1, keepdims=True)
    )

    grad_w_one, grad_w_two = format_first(first_all)
    second, second_other = after((second, second_other), grad_w_one, grad_w_two)
    grad_w_qkv, grad_w_out, small = format_second(me, second, second_other)
    summed = small[0] + small[1]

    def half(at, rows):
        return lax.dynamic_slice_in_dim(summed[at : at + rows], fsdp * (rows // 2), rows // 2).reshape(-1)

    grad_b_out = half(12, 6)
    return (
        layer_out,
        grad_tokens,
        half(24, 6),
        half(30, 6),
        half(0, 6),
        half(6, 6),
        grad_w_qkv,
        half(36, 18),
        grad_w_out,
        grad_b_out,
        grad_w_one,
        small[:, 18:24].reshape(-1),
        grad_w_two,
        grad_b_out,
    )


def solution(mesh):
    fine = Mesh(mesh.devices.reshape(SIZES), AXES)
    rows = P(AXES, None)
    vec = P("fsdp")
    mat = P("fsdp", None)
    return jax.shard_map(
        local,
        mesh=fine,
        in_specs=(
            rows, P(), rows, vec, vec, vec, vec, mat, vec, mat, vec, mat, vec, mat, vec,
        ),
        out_specs=(
            rows, rows, vec, vec, vec, vec, mat, vec, mat, vec, mat, vec, mat, vec,
        ),
        check_vma=False,
    )
```

```python
from functools import partial
import math

import jax
import jax.numpy as jnp
from jax import lax
from jax.experimental import pallas as pl
from jax.experimental.pallas import tpu as pltpu
from jax.sharding import Mesh, PartitionSpec as P

HEADS = 12
HEAD = 64
ROT = 16
D = 768
FF = 3072
BLK = 128
EPS = 1e-05
MASKED = -1e30
FLOOR = -1e20

AXES = ("z", "xh", "y", "core", "fsdp")
SIZES = (4, 2, 4, 2, 2)
CTX = ("z", "xh", "y", "core")
TEAM = ("core", "fsdp")
KEYS = ("z", "xh")
GROUPS = ("z", "xh", "y")

NH = 1
TH = 3
HW = TH * HEAD
KW = NH * HEAD
TEAM_ROWS = 512
NQ = 16
NK = 32
QT = 2
FQT = 4
CH = 4
PAIR = 2
FPAIR = 2
UNROLL = 8
BF = jnp.bfloat16
F32 = jnp.float32
VMEM_LIMIT = 56 * 1024 * 1024


def _sort_keys(kv_ref, ksrc, kvt, kn):
    def step(r, _):
        src = ksrc[r]
        at = pl.multiple_of((src % 4) * BLK, BLK)
        to = pl.multiple_of(r * BLK, BLK)
        blk = kv_ref[src // 4, :, pl.ds(at, BLK)]
        kvt[:, pl.ds(to, BLK)] = blk
        for h in range(NH):
            kn[h, pl.ds(to, BLK), :] = blk[2 * HEAD * h : 2 * HEAD * (h + 1)].T
        return 0

    lax.fori_loop(0, NK, step, 0, unroll=UNROLL)


def _head_rows(head):
    return slice(2 * HEAD * head, 2 * HEAD * (head + 1))


def _tile_columns(ref, qsrc, t, rows, qt):
    parts = []
    for i in range(qt):
        src = qsrc[t * qt + i]
        at = pl.multiple_of((src % 4) * BLK, BLK)
        parts.append(ref[src // 4, rows, pl.ds(at, BLK)])
    return jnp.concatenate(parts, axis=1)


def _allowed(kpos, qpos, t, c, qt):
    row = lax.broadcasted_iota(jnp.int32, (BLK, qt * BLK), 0)
    col = lax.broadcasted_iota(jnp.int32, (BLK, BLK), 1)
    query = jnp.concatenate([qpos[t * qt + i] * BLK + col for i in range(qt)], axis=1)
    return jnp.concatenate([kpos[c * CH + i] * BLK + row <= query for i in range(CH)], axis=0)


def _forward(head, qsrc, qpos, ksrc, kpos, nfull, nall, qd_ref, kv_ref, o_ref, kvt, kn):
    _sort_keys(kv_ref, ksrc, kvt, kn)
    width = FQT * BLK

    def tile(t, _):
        blk = _tile_columns(qd_ref, qsrc, t, _head_rows(head), FQT)
        half = lax.broadcasted_iota(jnp.int32, (2 * HEAD, width), 0) < HEAD
        zero = jnp.zeros((2 * HEAD, width), BF)
        queries = [
            jnp.where(half, blk[2 * HEAD * h : 2 * HEAD * (h + 1)], zero) for h in range(NH)
        ]

        def chunk(masked, step, c, carry):
            rows = step * CH * BLK
            at = pl.multiple_of(c * rows, rows)
            out = []
            if masked:
                ok = _allowed(kpos, qpos, t, c, FQT)
            for h in range(NH):
                m, l, acc = carry[h]
                s = jnp.dot(kn[h, pl.ds(at, rows), :], queries[h], preferred_element_type=F32)
                if masked:
                    s = jnp.where(ok, s, MASKED)
                new = jnp.maximum(m, jnp.max(s, axis=0, keepdims=True))
                p = jnp.exp(s - new)
                fade = jnp.exp(m - new)
                l = l * fade + jnp.sum(p, axis=0, keepdims=True)
                v = kvt[2 * HEAD * h + HEAD : 2 * HEAD * (h + 1), pl.ds(at, rows)]
                acc = acc * fade + jnp.dot(v, p.astype(BF), preferred_element_type=F32)
                out.append((new, l, acc))
            return tuple(out)

        start = tuple(
            (
                jnp.full((1, width), FLOOR, F32),
                jnp.zeros((1, width), F32),
                jnp.zeros((HEAD, width), F32),
            )
            for _ in range(NH)
        )
        wide = nfull[t] // FPAIR
        state = lax.fori_loop(0, wide, partial(chunk, False, FPAIR), start)
        state = lax.fori_loop(wide * FPAIR, nfull[t], partial(chunk, False, 1), state)
        state = lax.fori_loop(nfull[t], nall[t], partial(chunk, True, 1), state)
        stats = []
        for h in range(NH):
            m, l, acc = state[h]
            some = l > 0.0
            safe = jnp.where(some, l, 1.0)
            o = (acc / safe).astype(BF)
            lse = jnp.where(some, m + jnp.log(safe), FLOOR)
            hi = lse.astype(BF)
            rest = lse - hi.astype(F32)
            mid = rest.astype(BF)
            low = (rest - mid.astype(F32)).astype(BF)
            stats += [hi.astype(F32), mid.astype(F32), low.astype(F32)]
            for i in range(FQT):
                src = qsrc[t * FQT + i]
                at = pl.multiple_of((src % 4) * BLK, BLK)
                o_ref[src // 4, HEAD * h : HEAD * (h + 1), pl.ds(at, BLK)] = o[:, i * BLK : (i + 1) * BLK]
        stats = jnp.concatenate(stats + [jnp.zeros((16 - 3 * NH, width), F32)], axis=0).astype(BF)
        for i in range(FQT):
            src = qsrc[t * FQT + i]
            at = pl.multiple_of((src % 4) * BLK, BLK)
            o_ref[src // 4, KW : KW + 16, pl.ds(at, BLK)] = stats[:, i * BLK : (i + 1) * BLK]
        return 0

    lax.fori_loop(0, NQ // FQT, tile, 0)


def _row_stats(parts, src, grad):
    at = pl.multiple_of((src % 4) * BLK, BLK)
    outs, sums = [], []
    for i, ref in enumerate(parts):
        part = ref[(src // 4 + 4 - i) % 4, :, pl.ds(at, BLK)].astype(F32)
        outs.append(part[:HEAD])
        sums.append(part[HEAD : HEAD + 1] + part[HEAD + 1 : HEAD + 2] + part[HEAD + 2 : HEAD + 3])
    peak = jnp.maximum(jnp.maximum(sums[0], sums[1]), jnp.maximum(sums[2], sums[3]))
    shares = [jnp.exp(x - peak) for x in sums]
    total = shares[0] + shares[1] + shares[2] + shares[3]
    whole = sum(o * (x / total) for o, x in zip(outs, shares))
    return peak + jnp.log(total), jnp.sum(whole * grad, axis=0, keepdims=True)


def _backward(
    head, qsrc, qpos, ksrc, kpos, nfull, nall, qd_ref, kv_ref, o0, o1, o2, o3, dq_ref, dkv_ref,
    kvt, kn, acc, w1, w2, dq,
):
    _sort_keys(kv_ref, ksrc, kvt, kn)
    width = QT * BLK
    acc[...] = jnp.zeros_like(acc)

    def tile(t, _):
        blk = _tile_columns(qd_ref, qsrc, t, _head_rows(head), QT)
        stats = []
        for i in range(QT):
            grad = blk[HEAD:, i * BLK : (i + 1) * BLK].astype(F32)
            stats.append(_row_stats((o0, o1, o2, o3), qsrc[t * QT + i], grad))
        stats = [jnp.concatenate(part, axis=1) for part in zip(*stats)]
        top = lax.broadcasted_iota(jnp.int32, (2 * HEAD, width), 0) < HEAD
        left = lax.broadcasted_iota(jnp.int32, (width, 2 * HEAD), 1) < HEAD
        zero = jnp.zeros((2 * HEAD, width), BF)
        zero_t = jnp.zeros((width, 2 * HEAD), BF)
        for h in range(NH):
            both = blk[2 * HEAD * h : 2 * HEAD * (h + 1)]
            w1[h, :, :width] = jnp.where(top, both, zero)
            w1[h, :, width:] = jnp.where(top, zero, both)
            turned = both.T
            w2[h, :width, :] = jnp.where(left, turned, zero_t)
            w2[h, width:, :] = jnp.where(left, zero_t, turned)
        dq[...] = jnp.zeros_like(dq)

        def chunk(masked, step, c, _):
            rows = step * CH * BLK
            at = pl.multiple_of(c * rows, rows)
            if masked:
                ok = _allowed(kpos, qpos, t, c, QT)
            for h in range(NH):
                sd = jnp.dot(kn[h, pl.ds(at, rows), :], w1[h], preferred_element_type=F32)
                s = sd[:, :width]
                if masked:
                    s = jnp.where(ok, s, MASKED)
                p = jnp.exp(s - stats[0])
                ds = (p * (sd[:, width:] - stats[1])).astype(BF)
                pd = jnp.concatenate([ds, p.astype(BF)], axis=1)
                acc[h, pl.ds(at, rows), :] += jnp.dot(pd, w2[h], preferred_element_type=F32)
                k = kvt[2 * HEAD * h : 2 * HEAD * h + HEAD, pl.ds(at, rows)]
                dq[h] += jnp.dot(k, ds, preferred_element_type=F32)
            return 0

        wide = nfull[t] // PAIR
        lax.fori_loop(0, wide, partial(chunk, False, PAIR), 0)
        lax.fori_loop(wide * PAIR, nfull[t], partial(chunk, False, 1), 0)
        lax.fori_loop(nfull[t], nall[t], partial(chunk, True, 1), 0)
        for h in range(NH):
            out = (dq[h] * 0.125).astype(BF)
            for i in range(QT):
                src = qsrc[t * QT + i]
                at = pl.multiple_of((src % 4) * BLK, BLK)
                dq_ref[src // 4, HEAD * h : HEAD * (h + 1), pl.ds(at, BLK)] = out[:, i * BLK : (i + 1) * BLK]
        return 0

    lax.fori_loop(0, NQ // QT, tile, 0)

    def back(r, _):
        src = ksrc[r]
        at = pl.multiple_of((src % 4) * BLK, BLK)
        for h in range(NH):
            part = acc[h, pl.ds(pl.multiple_of(r * BLK, BLK), BLK), :].T.astype(BF)
            dkv_ref[src // 4, 2 * HEAD * h : 2 * HEAD * (h + 1), pl.ds(at, BLK)] = part
        return 0

    lax.fori_loop(0, NK, back, 0, unroll=UNROLL)


def _specs(n):
    return [pl.BlockSpec(memory_space=pltpu.VMEM)] * n


def attend_forward(head, plan, qd, kv):
    return pl.pallas_call(
        partial(_forward, head),
        out_shape=jax.ShapeDtypeStruct((4, KW + 16, TEAM_ROWS), BF),
        in_specs=[pl.BlockSpec(memory_space=pltpu.SMEM)] * 6 + _specs(2),
        out_specs=pl.BlockSpec(memory_space=pltpu.VMEM),
        scratch_shapes=[
            pltpu.VMEM((2 * KW, NK * BLK), BF),
            pltpu.VMEM((NH, NK * BLK, 2 * HEAD), BF),
        ],
        compiler_params=pltpu.CompilerParams(vmem_limit_bytes=VMEM_LIMIT),
        cost_estimate=pl.CostEstimate(flops=4 * NH * NQ * NK * BLK * BLK * HEAD, bytes_accessed=4 * NH * (NQ + NK) * BLK * BLK, transcendentals=NH * NQ * NK * BLK * BLK),
        name="attend_forward",
    )(*plan, qd, kv)


def attend_backward(head, plan, qd, kv, parts):
    width = QT * BLK
    return pl.pallas_call(
        partial(_backward, head),
        out_shape=(
            jax.ShapeDtypeStruct((4, KW, TEAM_ROWS), BF),
            jax.ShapeDtypeStruct((8, 2 * KW, TEAM_ROWS), BF),
        ),
        in_specs=[pl.BlockSpec(memory_space=pltpu.SMEM)] * 6 + _specs(6),
        out_specs=tuple(_specs(2)),
        scratch_shapes=[
            pltpu.VMEM((2 * KW, NK * BLK), BF),
            pltpu.VMEM((NH, NK * BLK, 2 * HEAD), BF),
            pltpu.VMEM((NH, NK * BLK, 2 * HEAD), F32),
            pltpu.VMEM((NH, 2 * HEAD, 2 * width), BF),
            pltpu.VMEM((NH, 2 * width, 2 * HEAD), BF),
            pltpu.VMEM((NH, HEAD, width), F32),
        ],
        compiler_params=pltpu.CompilerParams(vmem_limit_bytes=VMEM_LIMIT),
        cost_estimate=pl.CostEstimate(flops=10 * NH * NQ * NK * BLK * BLK * HEAD, bytes_accessed=8 * NH * (NQ + NK) * BLK * BLK, transcendentals=NH * NQ * NK * BLK * BLK),
        name="attend_backward",
    )(*plan, qd, kv, *parts)


def pick(table, index):
    ids = jnp.arange(table.shape[0], dtype=jnp.int32)
    return jnp.sum(jnp.where(index[:, None] == ids[None, :], table[None, :], 0), axis=1)


def in_order(pos):
    ids = jnp.arange(pos.shape[0], dtype=jnp.int32)
    rank = jnp.sum((pos[None, :] < pos[:, None]).astype(jnp.int32), axis=1)
    hit = rank[None, :] == ids[:, None]
    return (
        jnp.sum(jnp.where(hit, ids[None, :], 0), axis=1),
        jnp.sum(jnp.where(hit, pos[None, :], 0), axis=1),
    )


def make_plan(block_order, team, z, xh, y):
    rows = jnp.arange(4, dtype=jnp.int32) ^ team
    other = (y + jnp.arange(4, dtype=jnp.int32)) % 4
    mine = ((z * 2 + xh) * 4 + other)[:, None] * 4 + rows[None, :]
    theirs = (jnp.arange(8, dtype=jnp.int32) * 4 + y)[:, None] * 4 + rows[None, :]
    qsrc, qpos = in_order(pick(block_order, mine.reshape(-1)))
    ksrc, kpos = in_order(pick(block_order, theirs.reshape(-1)))

    def plan(qt):
        ends = qpos.reshape(NQ // qt, qt)
        below = jnp.sum((kpos[None, :] < ends[:, :1]).astype(jnp.int32), axis=1)
        upto = jnp.sum((kpos[None, :] <= ends[:, -1:]).astype(jnp.int32), axis=1)
        return (qsrc, qpos, ksrc, kpos, below // CH, (upto + CH - 1) // CH)

    return plan(FQT), plan(QT)


def from_y(x, i):
    return lax.ppermute(x, "y", [((d + i) % 4, d) for d in range(4)])


def to_y(x, i):
    return lax.ppermute(x, "y", [(d, (d + i) % 4) for d in range(4)])


def from_keys(x):
    return lax.all_to_all(jnp.broadcast_to(x[None], (8,) + x.shape), KEYS, 0, 0, tiled=True)


def to_keys(parts):
    return lax.all_to_all(parts, KEYS, 0, 0, tiled=True)


def after(values, *done):
    return lax.optimization_barrier((values, done))[0]


def swapped(x, axis):
    return lax.ppermute(x, axis, [(0, 1), (1, 0)])


def team_rows(x):
    pair = jnp.concatenate([x, swapped(x, "fsdp")])
    return jnp.concatenate([pair, swapped(pair, "core")])


def _format_first(all_ref, one_ref, two_ref):
    for i in range(16):
        block = all_ref[0, i, 0].astype(F32)
        one_ref[24 * i : 24 * (i + 1), :] = block[:24]
        two_ref[24 * i : 24 * (i + 1), :] = block[24:48]


def format_first(gathered):
    n = gathered.shape[1]
    return pl.pallas_call(
        _format_first,
        grid=(2, 2),
        out_shape=(
            jax.ShapeDtypeStruct((384, FF), F32),
            jax.ShapeDtypeStruct((FF // 2, D), F32),
        ),
        in_specs=[pl.BlockSpec((1, 16, 1, n, D), lambda zh, c: (zh, 0, c, 0, 0))],
        out_specs=(
            pl.BlockSpec((384, D), lambda zh, c: (0, zh * 2 + c)),
            pl.BlockSpec((384, D), lambda zh, c: (c * 2 + zh, 0)),
        ),
        compiler_params=pltpu.CompilerParams(vmem_limit_bytes=VMEM_LIMIT),
        name="format_first",
    )(gathered.reshape(2, 16, 2, n, D))


def _ordered(first, own, other):
    return jnp.where(first, own, other), jnp.where(first, other, own)


def _turn(x, cosine, sine):
    a, b = x[: ROT // 2], x[ROT // 2 : ROT]
    return jnp.concatenate([a * cosine - b * sine, b * cosine + a * sine, x[ROT:]], axis=0)


def _project(
    me, x_ref, dy_ref, wk_ref, wo_ref, wout_ref, own_ref, other_ref, cos_ref, sin_ref,
    n_ref, scale_ref, a_ref, m_ref, vec_ref, *heads,
):
    first = me[0] == 0
    lo, hi = _ordered(first, own_ref[...].astype(F32), other_ref[...].astype(F32))
    vec = jnp.concatenate([lo, hi], axis=1)
    vec_ref[...] = vec
    x = x_ref[...].astype(F32)
    centred = x - jnp.mean(x, axis=1, keepdims=True)
    scale = lax.rsqrt(jnp.mean(centred * centred, axis=1, keepdims=True) + EPS)
    n = centred * scale
    n_ref[...] = n
    scale_ref[...] = jnp.broadcast_to(scale, scale_ref.shape)
    a = n * vec[0:1] + vec[1:2]
    a_ref[...] = a.astype(BF)
    m_ref[...] = (n * vec[2:3] + vec[3:4]).astype(BF)
    keep, rest = _ordered(first, a[:, : D // 2], a[:, D // 2 :])
    qkv = jnp.dot(keep.astype(BF), wk_ref[...], preferred_element_type=F32)
    qkv = qkv + jnp.dot(rest.astype(BF), wo_ref[...], preferred_element_type=F32)
    bias = []
    for p in range(3):
        part = jnp.zeros((1, HW), F32)
        for j in range(4):
            b = p * 4 + j
            src = (lo, hi)[b // 6]
            row = 6 + (b % 6) // 2
            at = (b % 2) * HW
            part = part + jnp.where(me[1] == j, src[row : row + 1, at : at + HW], 0.0)
        bias.append(part)
    qkv = (qkv + jnp.concatenate(bias, axis=1)).T
    d_mixed = lax.dot_general(
        wout_ref[...], dy_ref[...], (((1,), (1,)), ((), ())), preferred_element_type=F32
    ).astype(BF)
    cosine, sine = cos_ref[...], sin_ref[...]
    for h in range(TH):
        kv_ref, qd_ref = heads[h], heads[TH].at[_head_rows(h)]
        rows = [slice(p * HW + h * HEAD, p * HW + (h + 1) * HEAD) for p in range(3)]
        qd_ref[:HEAD] = _turn(qkv[rows[0]], cosine, sine).astype(BF) * jnp.asarray(0.125, BF)
        qd_ref[HEAD:] = d_mixed[h * HEAD : (h + 1) * HEAD]
        kv_ref[:HEAD] = _turn(qkv[rows[1]], cosine, sine).astype(BF)
        kv_ref[HEAD:] = qkv[rows[2]].astype(BF)


def project(me, *args):
    return pl.pallas_call(
        _project,
        out_shape=(
            jax.ShapeDtypeStruct((TEAM_ROWS, D), F32),
            jax.ShapeDtypeStruct((TEAM_ROWS, 128), F32),
            jax.ShapeDtypeStruct((TEAM_ROWS, D), BF),
            jax.ShapeDtypeStruct((TEAM_ROWS, D), BF),
            jax.ShapeDtypeStruct((9, D), F32),
        )
        + (jax.ShapeDtypeStruct((2 * HEAD, TEAM_ROWS), BF),) * TH
        + (jax.ShapeDtypeStruct((2 * HW, TEAM_ROWS), BF),),
        in_specs=[pl.BlockSpec(memory_space=pltpu.SMEM)] + _specs(9),
        out_specs=tuple(_specs(6 + TH)),
        compiler_params=pltpu.CompilerParams(vmem_limit_bytes=VMEM_LIMIT),
        name="project",
    )(me, *args)


def _nt(a, b):
    return lax.dot_general(a, b, (((1,), (1,)), ((), ())), preferred_element_type=F32)


def _tn(a, b):
    return lax.dot_general(a, b, (((0,), (0,)), ((), ())), preferred_element_type=F32)


def _feed_forward(
    me, m_ref, keep_ref, rest_ref, two_ref, dy_ref, bias_ref, n_ref, first_ref, out_ref, dh_ref, early_ref
):
    lower = me[0] == 0
    m = m_ref[...].astype(F32)
    left, right = _ordered(lower, m[:, : D // 2], m[:, D // 2 :])
    left, right = left.astype(BF), right.astype(BF)
    dy = dy_ref[...]
    x = jnp.dot(left, keep_ref[...], preferred_element_type=F32)
    x = x + jnp.dot(right, rest_ref[...], preferred_element_type=F32) + bias_ref[...]
    phi = 0.5 * (1.0 + lax.erf(x * math.sqrt(0.5)))
    act = (x * phi).astype(BF)
    slope = phi + x * jnp.exp(-0.5 * x * x) * (1.0 / math.sqrt(2.0 * math.pi))
    out_ref[...] = jnp.dot(act, two_ref[...], preferred_element_type=F32)
    hidden = (_nt(dy, two_ref[...]) * slope).astype(BF)
    dh = jnp.concatenate(
        _ordered(lower, _nt(hidden, keep_ref[...]), _nt(hidden, rest_ref[...])), axis=1
    )
    dh_ref[...] = dh
    early_ref[0:1, :] = jnp.sum(dh * n_ref[...], axis=0, keepdims=True)
    early_ref[1:2, :] = jnp.sum(dh, axis=0, keepdims=True)
    early_ref[2:3, :] = jnp.sum(dy[:BLK].astype(F32), axis=0, keepdims=True)
    early_ref[3:4, :] = jnp.sum(hidden.astype(F32), axis=0, keepdims=True)
    one = jnp.concatenate(_ordered(lower, _tn(left, hidden), _tn(right, hidden)), axis=0)
    two = _tn(act, dy)
    for g in range(32):
        rows = slice(24 * g, 24 * (g + 1))
        first_ref[g] = jnp.concatenate([one[rows], two[rows]], axis=0).astype(BF)


def feed_forward(me, *args):
    return pl.pallas_call(
        _feed_forward,
        out_shape=(
            jax.ShapeDtypeStruct((32, 48, D), BF),
            jax.ShapeDtypeStruct((TEAM_ROWS, D), F32),
            jax.ShapeDtypeStruct((TEAM_ROWS, D), F32),
            jax.ShapeDtypeStruct((4, D), F32),
        ),
        in_specs=[pl.BlockSpec(memory_space=pltpu.SMEM)] + _specs(7),
        out_specs=tuple(_specs(4)),
        compiler_params=pltpu.CompilerParams(vmem_limit_bytes=VMEM_LIMIT),
        name="feed_forward",
    )(me, *args)


SLOT = 128


def _tail(
    me, dq_ref, dkv0_ref, dkv_ref, cos_ref, sin_ref, a_ref, n_ref, dy_ref, mixed_ref,
    w_ref, early_ref, second_ref, dh_ref, small,
):
    cosine, sine = cos_ref[...], -sin_ref[...]
    keys = [dkv0_ref[...], dkv_ref[: 2 * HEAD], dkv_ref[2 * HEAD :]]
    parts = [_turn(dq_ref[h * HEAD : (h + 1) * HEAD], cosine, sine) for h in range(TH)]
    parts += [_turn(x[:HEAD], cosine, sine) for x in keys]
    parts += [x[HEAD:] for x in keys]
    turned = jnp.concatenate(parts, axis=0).astype(BF)
    grads = jnp.concatenate(
        [
            jnp.dot(turned, a_ref[...], preferred_element_type=F32),
            jnp.dot(mixed_ref[...], dy_ref[...], preferred_element_type=F32),
        ],
        axis=0,
    ).T
    rows = turned.astype(F32).T
    dh = lax.dot_general(
        rows.astype(BF), w_ref[...], (((1,), (1,)), ((), ())), preferred_element_type=F32
    )
    dh_ref[...] = dh
    vectors = [early_ref[i : i + 1] for i in range(4)]
    vectors.append(jnp.sum(dh * n_ref[...], axis=0, keepdims=True))
    vectors.append(jnp.sum(dh, axis=0, keepdims=True))
    bias = jnp.sum(rows, axis=0, keepdims=True)
    for p in range(3):
        part = bias[:, p * HW : (p + 1) * HW]
        vectors.append(
            jnp.concatenate([jnp.where(me[1] == j, part, 0.0) for j in range(4)], axis=1)
        )
    small[...] = jnp.zeros_like(small)
    for v, vector in enumerate(vectors):
        for i in range(6):
            at = v * 6 + i
            small[at % 32, at // 32 : at // 32 + 1, :] = vector[:, i * SLOT : (i + 1) * SLOT]
    for g in range(32):
        second_ref[g, :, :D] = grads[24 * g : 24 * (g + 1)].astype(BF)
        second_ref[g, :, D:] = small[g].astype(BF)


def tail(me, *args):
    return pl.pallas_call(
        _tail,
        out_shape=(
            jax.ShapeDtypeStruct((32, 24, D + SLOT), BF),
            jax.ShapeDtypeStruct((TEAM_ROWS, D), F32),
        ),
        in_specs=[pl.BlockSpec(memory_space=pltpu.SMEM)] + _specs(11),
        out_specs=tuple(_specs(2)),
        scratch_shapes=[pltpu.VMEM((32, 24, SLOT), F32)],
        compiler_params=pltpu.CompilerParams(vmem_limit_bytes=VMEM_LIMIT),
        name="tail",
    )(me, *args)


def _format_second(me, own_ref, other_ref, qkv_ref, out_ref, small_ref):
    first = me[2] == 0
    turned = [[], []]
    for zh in range(2):
        for i in range(16):
            g = zh * 16 + i
            pair = _ordered(first, own_ref[g].astype(F32), other_ref[g].astype(F32))
            for c, block in enumerate(pair):
                h = zh * 2 + c
                for p in range(3):
                    at = p * D + h * HW
                    qkv_ref[24 * i : 24 * (i + 1), at : at + HW] = block[:, p * HW : (p + 1) * HW]
                turned[c].append(block[:, 3 * HW : D])
                for slot in range(2):
                    small_ref[c, slot * 32 + g : slot * 32 + g + 1, :] = block[slot : slot + 1, D:]
    for c in range(2):
        out_ref[c * HW : (c + 1) * HW, :] = jnp.concatenate(turned[c], axis=0).T


def format_second(me, own, other):
    return pl.pallas_call(
        _format_second,
        out_shape=(
            jax.ShapeDtypeStruct((384, 3 * D), F32),
            jax.ShapeDtypeStruct((384, D), F32),
            jax.ShapeDtypeStruct((2, 64, SLOT), F32),
        ),
        in_specs=[pl.BlockSpec(memory_space=pltpu.SMEM)] + _specs(2),
        out_specs=tuple(_specs(3)),
        compiler_params=pltpu.CompilerParams(vmem_limit_bytes=VMEM_LIMIT),
        name="format_second",
    )(me, own, other)


def dot(a, b, dims):
    return lax.dot_general(a, b, (dims, ((), ())), preferred_element_type=F32)


def local(
    tokens,
    block_order,
    cotangent,
    ln_gain_attn,
    ln_bias_attn,
    ln_gain_mlp,
    ln_bias_mlp,
    w_qkv,
    b_qkv,
    w_out,
    b_out,
    w_fc1,
    b_fc1,
    w_fc2,
    b_fc2,
):
    z, xh, y, core, fsdp = (lax.axis_index(a) for a in AXES)
    team = core * 2 + fsdp
    mine = fsdp * 2 + core
    theirs = (1 - fsdp) * 2 + core
    group = (z * 2 + xh) * 4 + y

    def columns(w, which, width):
        return lax.dynamic_slice_in_dim(w, which * width, width, axis=1)

    def qkv_columns(w, which):
        return jnp.concatenate(
            [columns(w[:, i * D : (i + 1) * D], which, HW) for i in range(3)], axis=1
        )

    def ordered(keep, other):
        return (jnp.where(fsdp == 0, keep, other), jnp.where(fsdp == 0, other, keep))

    me = jnp.stack([fsdp, mine, core]).astype(jnp.int32)

    x4 = team_rows(tokens)
    w_keep = qkv_columns(w_qkv, mine)
    w_rest = swapped(qkv_columns(w_qkv, theirs), "fsdp")
    dy4 = team_rows(cotangent)
    vectors = jnp.concatenate(
        [
            v.reshape(-1, 384)
            for v in (ln_gain_attn, ln_bias_attn, ln_gain_mlp, ln_bias_mlp, b_out, b_fc2, b_qkv)
        ]
    )
    w_o = lax.dynamic_slice_in_dim(w_out, core * HW, HW, axis=0)
    one_rest = swapped(columns(w_fc1, theirs, D), "fsdp")
    later_one, later_two, later_bias = after((w_fc1, w_fc2, b_fc1), x4)
    one_keep = columns(later_one, mine, D)
    w_two = lax.dynamic_slice_in_dim(later_two, core * D, D, axis=0)
    b_one = lax.dynamic_slice_in_dim(later_bias, core * D, D, axis=0).astype(F32)[None]

    fplan, bplan = make_plan(block_order, team, z, xh, y)

    anchors = pick(block_order, group * 4 + (jnp.arange(4, dtype=jnp.int32) ^ team))
    places = (anchors[:, None] * BLK + jnp.arange(BLK, dtype=jnp.int32)[None, :]).reshape(-1)
    frequency = jnp.exp(jnp.arange(ROT // 2, dtype=F32) * (-2.0 * math.log(10000.0) / ROT))
    angles = frequency[:, None] * places.astype(F32)[None, :]
    cosine, sine = jnp.cos(angles), jnp.sin(angles)

    n, scale, a_attn, a_mlp, vec, *heads = project(
        me, x4, dy4, w_keep, w_rest, w_o, vectors, swapped(vectors, "fsdp"), cosine, sine
    )
    *kvs, qd = heads
    kv_0, kv_1 = from_keys(kvs[0]), from_keys(kvs[1])
    qd_all = jnp.stack([qd] + [from_y(qd, i) for i in range(1, 4)])

    first, out_part, dh_mlp, early = feed_forward(
        me, a_mlp, one_keep, one_rest, w_two, dy4, b_one, n
    )

    def to_owner(part):
        pairs = []
        for at in range(8):
            zz, f = at // 2, at % 2
            if f == 0 and zz >= 2:
                pairs.append((at, (zz - 2) * 2 + 1))
            elif f == 1 and zz < 2:
                pairs.append((at, (zz + 2) * 2))
            else:
                pairs.append((at, at))
        return lax.ppermute(part, ("z", "fsdp"), pairs)

    def spread(out, *done):
        return after([out] + [from_y(out, i) for i in range(1, 4)], *done)

    def merged(parts):
        own = jnp.stack([part[-i % 4] for i, part in enumerate(parts)]).astype(F32)
        lse = jnp.sum(own[:, HEAD : HEAD + 3], axis=1)
        share = jnp.exp(lse - jnp.max(lse, axis=0))
        share = share / jnp.sum(share, axis=0)
        return jnp.sum(own[:, :HEAD] * share[:, None, :], axis=0).astype(BF)

    kv_0, fplan = after((kv_0, fplan), first)
    out_0 = attend_forward(0, fplan, qd_all, kv_0)
    kv_1, kv_2 = after((kv_1, kvs[2]), out_0)
    kv_2 = from_keys(kv_2)
    out_1 = attend_forward(1, after(fplan, out_0), qd_all, kv_1)
    first = lax.all_to_all(after(first, out_1), GROUPS, 0, 0, tiled=True)
    kv_2 = after(kv_2, out_1)
    out_2 = attend_forward(2, after(fplan, out_1), qd_all, kv_2)
    parts_0 = spread(out_0, out_2)
    raw_0 = attend_backward(0, after(bplan, out_2), qd_all, kv_0, parts_0)
    parts_1 = spread(out_1, raw_0)
    first = jnp.sum(after(first, raw_0).astype(F32), axis=0)
    raw_1 = attend_backward(1, after(bplan, raw_0, first), qd_all, kv_1, parts_1)
    parts_2 = spread(out_2, raw_1)
    dkv_0 = jnp.sum(after(to_keys(raw_0[1]), raw_1).astype(F32), axis=0)
    raw_2 = attend_backward(2, after(bplan, raw_1, dkv_0), qd_all, kv_2, parts_2)
    dkv = to_keys(jnp.concatenate([raw_1[1], raw_2[1]], axis=1))
    dkv = jnp.sum(dkv.astype(F32), axis=0)
    dq = jnp.concatenate([raw_0[0], raw_1[0], raw_2[0]], axis=1)
    dq = [dq[0]] + [to_y(dq[i], i) for i in range(1, 4)]
    dq = sum(part.astype(F32) for part in dq)
    all_parts = after((parts_0, parts_1, parts_2), raw_2)
    mixed = jnp.concatenate([merged(parts) for parts in all_parts])

    first = jnp.concatenate([to_owner(first[:24].astype(BF)), first[24:].astype(BF)], axis=0)
    first_all = lax.all_gather(first, CTX, axis=0, tiled=False)

    w_q = jnp.concatenate(ordered(w_keep, w_rest))
    second, dh_attn = tail(
        me,
        dq,
        dkv_0,
        dkv,
        cosine,
        sine,
        a_attn,
        n,
        dy4,
        mixed,
        w_q,
        early,
    )
    second = jnp.sum(lax.all_to_all(second, GROUPS, 0, 0, tiled=True).astype(F32), axis=0)
    second = second.astype(BF)
    second = jnp.concatenate([to_owner(second[:, : 3 * HW]), second[:, 3 * HW :]], axis=1)
    sent = jnp.broadcast_to(second[None], (32,) + second.shape)
    second = lax.all_to_all(sent, GROUPS, 0, 0, tiled=True)
    second_other = swapped(second, "core")
    rows = swapped(second[:, :2, D:], "fsdp")
    rows = rows.astype(F32) + swapped(rows, "core").astype(F32)
    rows = jnp.concatenate([rows[:, 0], rows[:, 1]], axis=0)

    out_part = out_part + dot(mixed, w_o, ((0,), (0,)))
    dn_part = dh_attn * vec[0:1] + dh_mlp * vec[2:3]
    both = jnp.concatenate([out_part, dn_part], axis=1).reshape(4, BLK, 2 * D)
    both = both[:2] + swapped(both[2:].astype(BF), "core").astype(F32)
    both = both[0] + swapped(both[1].astype(BF), "fsdp").astype(F32)
    layer_out = (tokens.astype(F32) + both[:, :D] + vec[4:5] + vec[5:6]).astype(BF)
    dn = both[:, D:]
    grad_tokens = cotangent.astype(F32) + scale[:BLK, :1] * (
        dn
        - jnp.mean(dn, axis=1, keepdims=True)
        - n[:BLK] * jnp.mean(dn * n[:BLK], axis=1, keepdims=True)
    )

    grad_w_one, grad_w_two = format_first(first_all)
    second, second_other = after((second, second_other), grad_w_one, grad_w_two)
    grad_w_qkv, grad_w_out, small = format_second(me, second, second_other)
    summed = small[0] + small[1] + rows

    def half(at, rows):
        return lax.dynamic_slice_in_dim(summed[at : at + rows], fsdp * (rows // 2), rows // 2).reshape(-1)

    grad_b_out = half(12, 6)
    return (
        layer_out,
        grad_tokens,
        half(24, 6),
        half(30, 6),
        half(0, 6),
        half(6, 6),
        grad_w_qkv,
        half(36, 18),
        grad_w_out,
        grad_b_out,
        grad_w_one,
        small[:, 18:24].reshape(-1),
        grad_w_two,
        grad_b_out,
    )


def solution(mesh):
    fine = Mesh(mesh.devices.reshape(SIZES), AXES)
    rows = P(AXES, None)
    vec = P("fsdp")
    mat = P("fsdp", None)
    return jax.shard_map(
        local,
        mesh=fine,
        in_specs=(
            rows, P(), rows, vec, vec, vec, vec, mat, vec, mat, vec, mat, vec, mat, vec,
        ),
        out_specs=(
            rows, rows, vec, vec, vec, vec, mat, vec, mat, vec, mat, vec, mat, vec,
        ),
        check_vma=False,
    )
```
